32 devices in a mesh: section: 2 (over core), row: 8 (over z, x), col: 2 (over y).
Axes of the slice: x: 2, y: 2, z: 4, core: 2. Of those that a mesh axis runs over, the one named last changes fastest.
Arguments:
- prior_root: float32 [512, 32, 2, 256], P(None, None, 'col'), may hold values from -0.08 to 4, as said below
- observations: float32 [2, 1024, 32, 2, 256], P('section', 'row', None, 'col'), may hold values from -0.5 to 0.5
- live_rows: int32 [2, 8], P('section', 'row'), may hold values from 1 to 128, 640 in all within a row
Outputs:
- r_slab: float32 [2, 512, 32, 2, 256], P('section', 'row', None, 'col')
The draws below stay inside these ranges and needn't reach their ends.
Inputs may be any that keep to these rules, and one draw needn't show every extreme that they name: `prior_root`: zero where the global column is below the row, positive on the diagonal. `live_rows`: within one arc group the counts sum to 640; the largest count of each arc group is 128.
All inputs are finite; a program needn't handle non-finite values.
Results may differ from the reference program's by a relative error of at most 0.0001.
Values sent between devices are 32-bit elements; how exact they have to be, the bound alone decides.
No kernel may reach another device: no remote copies, remote signals or barrier semaphores. Data moves between devices by JAX's collectives and lax.ppermute only.
A program may use at most 192 MiB of HBM per device.

```python
import math
import jax
import jax.numpy as jnp
import numpy as np
from jax import lax

PANEL = 256
OBS_DEV = 128
RROWS = 512
CYC = 32
OBSROWS = 1024
GROUPS = 2
N_ROW = 8
N_COL = 2


def draw_prior_root(key, part):
    key_diag, key_upper = jax.random.split(key)
    full_shape = (RROWS, CYC, N_COL, PANEL)
    cycle_ids = jnp.arange(CYC, dtype=jnp.int32)[None, :, None, None]
    device_ids = jnp.arange(N_COL, dtype=jnp.int32)[None, None, :, None]
    within_ids = jnp.arange(PANEL, dtype=jnp.int32)[None, None, None, :]
    column_ids = (cycle_ids * N_COL + device_ids) * PANEL + within_ids
    row_ids = jnp.arange(RROWS, dtype=jnp.int32)[:, None, None, None]
    diagonal = jax.random.uniform(key_diag, full_shape, jnp.float32, 1.0, 2.0)
    upper_part = 0.02 * jax.random.truncated_normal(key_upper, -4.0, 4.0, full_shape, jnp.float32)
    zeros_part = jnp.zeros(full_shape, jnp.float32)
    values = jnp.where(column_ids == row_ids, diagonal, jnp.where(column_ids > row_ids, upper_part, zeros_part))
    return values.astype(jnp.float32)


def block_scale(rng, dims, pieces, least, largest):
    level, own = 1.0, jax.random.fold_in(rng, 6)
    for position, parts in pieces:
        heights = jnp.exp(jax.random.uniform(jax.random.fold_in(own, position), (parts,), jnp.float32, least / len(pieces), largest / len(pieces)))
        level = level * jnp.repeat(heights, dims[position] // parts).reshape([-1 if axis == position else 1 for axis in range(len(dims))])
    return level


def split_up(number_of, total, limit, slope):
    portions = [(1 << 20) // math.isqrt(rank ** slope) + 1 for rank in range(2, number_of + 1)]
    surplus, given = total - limit - (number_of - 1), [1] * (number_of - 1)
    while surplus > 0:
        candidates = [i for i in range(number_of - 1) if given[i] < limit]
        pool, remaining = sum([portions[i] for i in candidates]), surplus
        for i in candidates:
            addition = min(limit - given[i], max(1, remaining * portions[i] // pool), surplus)
            given[i] = given[i] + addition
            surplus = surplus - addition
    return np.array([limit] + given)


def ragged(stream_key, amount, total, bound, slope):
    if amount == 2:
        one = jax.random.randint(stream_key, (), max(1, total - bound), min(bound, total - 1) + 1)
        return jnp.stack([one, total - one])
    sizes = jnp.asarray(split_up(amount, total, bound, slope), jnp.int32)
    pairs = (amount - 1) // 2
    giver, receiver = sizes[1:1 + 2 * pairs:2], sizes[2:2 + 2 * pairs:2]
    margin = jnp.minimum(giver - 1, bound - receiver)
    shifted = jax.random.randint(jax.random.fold_in(stream_key, 1), (pairs,), 0, 1 << 20) % (margin + 1)
    sizes = sizes.at[1:1 + 2 * pairs:2].set(giver - shifted).at[2:2 + 2 * pairs:2].set(receiver + shifted)
    return sizes[jax.random.permutation(jax.random.fold_in(stream_key, 2), amount)]


def noise(rng, dims, spread, most, cuts=(), kind=jnp.bfloat16):
    array = spread * jax.random.normal(rng, dims, jnp.float32)
    if cuts:
        array = array * block_scale(rng, dims, cuts, -0.22, 0.18)
    return jnp.clip(array, -most, most).astype(kind)


def setup_inputs(seed: int = 0) -> dict:
    key_of = jax.random.split(jax.random.key(seed), 4)
    return {
        "prior_root": draw_prior_root(jax.random.fold_in(key_of[3], 71), 0),
        "observations": noise(key_of[1], (GROUPS, OBSROWS, CYC, N_COL, PANEL), OBS_DEV ** -0.5, 0.5, ((0, 2), (1, 8), (3, 2)), jnp.float32),
        "live_rows": jax.vmap(lambda own: ragged(own, N_ROW, OBSROWS * 5 // 8, OBS_DEV, 2))(jax.random.split(key_of[2], GROUPS)).reshape((GROUPS, N_ROW)).astype(jnp.int32),
    }


def gram_product(left, right):
    return lax.dot_general(left.astype(jnp.float32), right.astype(jnp.float32), (((0,), (0,)), ((), ())), precision=lax.Precision.HIGHEST, preferred_element_type=jnp.float32)

def reference(prior_root, observations, live_rows):
    width = CYC * N_COL * PANEL
    prior_rows = prior_root.reshape(RROWS, width)
    column_ids = jnp.arange(width, dtype=jnp.int32)
    row_ids = jnp.arange(RROWS, dtype=jnp.int32)
    slot_ids = jnp.arange(OBS_DEV, dtype=jnp.int32)
    results = []
    for group in range(GROUPS):
        observed = observations[group].reshape(OBSROWS, width)
        live_mask = (slot_ids[None, :] < live_rows[group][:, None]).reshape(OBSROWS)
        observed = jnp.where(live_mask[:, None], observed, jnp.zeros_like(observed))
        information = gram_product(prior_rows[:, :RROWS], prior_rows) + gram_product(observed[:, :RROWS], observed)
        lower_factor = jnp.linalg.cholesky(information[:, :RROWS])
        slab_rows = lax.linalg.triangular_solve(lower_factor, information, left_side=True, lower=True)
        slab_rows = jnp.where(column_ids[None, :] >= row_ids[:, None], slab_rows, jnp.zeros_like(slab_rows))
        results.append(slab_rows)
        prior_rows = slab_rows
    return jnp.stack(results).reshape(GROUPS, RROWS, CYC, N_COL, PANEL)
```

```python
import functools

import jax
import jax.numpy as jnp
from jax import lax
from jax.experimental import pallas as pl
from jax.experimental.pallas import tpu as pltpu
from jax.sharding import PartitionSpec as P

LANES = 128
TALL = 16
GROUP = 8
SPOTS = 10
VMEM_BYTES = 56 * 2**20


def dot(left, right, contract_left, contract_right):
    return lax.dot_general(
        left,
        right,
        (((contract_left,), (contract_right,)), ((), ())),
        precision=lax.Precision.HIGHEST,
        preferred_element_type=jnp.float32,
    )


def spread(row, shape):
    return jnp.broadcast_to(row, shape)


def factor_block(work_ref):
    size = work_ref.shape[0]
    tile = (8, LANES)
    row_ids = lax.broadcasted_iota(jnp.int32, tile, 0)
    for first in range(0, size, TALL):
        middle, end = first + 8, first + TALL
        top = [work_ref[first:middle, t * LANES : (t + 1) * LANES] for t in range(2)]
        low = [work_ref[middle:end, t * LANES : (t + 1) * LANES] for t in range(2)]
        top_col = [spread(top[0][:, first + k : first + k + 1], tile) for k in range(TALL)]
        low_col = [spread(low[0][:, first + k : first + k + 1], tile) for k in range(TALL)]
        top_pivot = jnp.ones(tile, jnp.float32)
        low_pivot = jnp.ones(tile, jnp.float32)
        for step in range(TALL):
            if step < 8:
                pivot = spread(top_col[step][step : step + 1], tile)
                inverse = 1.0 / pivot
                top_by = jnp.where(row_ids > step, top_col[step] * inverse, 0.0)
                low_by = low_col[step] * inverse
                top_pivot = jnp.where(row_ids == step, pivot, top_pivot)
                for k in range(step + 1, TALL):
                    lead = spread(top_col[k][step : step + 1], tile)
                    top_col[k] = top_col[k] - top_by * lead
                    low_col[k] = low_col[k] - low_by * lead
                for t in range(2):
                    lead = spread(top[t][step : step + 1], tile)
                    top[t] = top[t] - top_by * lead
                    low[t] = low[t] - low_by * lead
            else:
                at = step - 8
                pivot = spread(low_col[step][at : at + 1], tile)
                low_by = jnp.where(row_ids > at, low_col[step] * (1.0 / pivot), 0.0)
                low_pivot = jnp.where(row_ids == at, pivot, low_pivot)
                for k in range(step + 1, TALL):
                    low_col[k] = low_col[k] - low_by * spread(low_col[k][at : at + 1], tile)
                for t in range(2):
                    low[t] = low[t] - low_by * spread(low[t][at : at + 1], tile)
        top_scale, low_scale = lax.rsqrt(top_pivot), lax.rsqrt(low_pivot)
        for t in range(2):
            work_ref[first:middle, t * LANES : (t + 1) * LANES] = top[t] * top_scale
            work_ref[middle:end, t * LANES : (t + 1) * LANES] = low[t] * low_scale
        if end < size:
            done = work_ref[first:end, :]
            change = dot(done[:, :LANES], done, 0, 0)
            work_ref[end:, :] = work_ref[end:, :] - change[end:, :]


def factor_kernel(own_ref, other_ref, inverse_ref, info_ref, work_ref):
    size = own_ref.shape[0]
    ids = [lax.broadcasted_iota(jnp.int32, (LANES, LANES), axis) for axis in range(2)]
    eye = (ids[0] == ids[1]).astype(jnp.float32)
    info_ref[...] = own_ref[...] + other_ref[...]
    inverse_ref[...] = jnp.zeros_like(inverse_ref)
    for start in range(0, size, LANES):
        end = start + LANES
        work_ref[:, :LANES] = info_ref[start:end, start:end]
        work_ref[:, LANES:] = eye
        factor_block(work_ref)
        block = work_ref[:, LANES:]
        if start:
            inverse_ref[start:end, :start] = dot(block, inverse_ref[start:end, :start], 1, 0)
        inverse_ref[start:end, start:end] = block
        if end < size:
            upper = dot(block, info_ref[start:end, end:], 1, 0)
            info_ref[end:, end:] = info_ref[end:, end:] - dot(upper, upper, 0, 0)
            inverse_ref[end:, :end] = inverse_ref[end:, :end] - dot(
                upper, inverse_ref[start:end, :end], 0, 0
            )


def vmem_spec():
    return pl.BlockSpec(memory_space=pltpu.VMEM)


def params():
    return pltpu.CompilerParams(vmem_limit_bytes=VMEM_BYTES)


def shape_of(*shape):
    return jax.ShapeDtypeStruct(shape, jnp.float32)


def factor(own, other):
    size = own.shape[0]
    return pl.pallas_call(
        factor_kernel,
        out_shape=shape_of(size, size),
        in_specs=[vmem_spec()] * 2,
        out_specs=vmem_spec(),
        scratch_shapes=[
            pltpu.VMEM((size, size), jnp.float32),
            pltpu.VMEM((LANES, 2 * LANES), jnp.float32),
        ],
        compiler_params=params(),
        name="factor",
    )(own, other)


def panel_kernel(count, spot_ref, near_ref, *refs):
    near_prior, far_prior, rows_ref, prior_ref, gram_ref = refs[-5:]
    parts = refs[:-5]
    width = near_prior.shape[1]
    col, section = spot_ref[0], spot_ref[1]
    near_at = pl.ds(pl.multiple_of(col * width, width), width)
    far_at = pl.ds(pl.multiple_of((1 - col) * width, width), width)
    slots = near_ref.shape[0] * 2 // count
    near_next, far_here, far_next = parts
    for i in range(count // 2):
        here, beside = 2 * i * slots, (2 * i + 1) * slots
        piece = slice(i * slots, (i + 1) * slots)
        rows_ref[here : here + slots, near_at] = near_ref[piece]
        rows_ref[beside : beside + slots, near_at] = near_next[piece]
        rows_ref[here : here + slots, far_at] = far_here[piece]
        rows_ref[beside : beside + slots, far_at] = far_next[piece]
    keep = (section == 0).astype(jnp.float32)
    prior_ref[:, near_at] = near_prior[...] * keep
    prior_ref[:, far_at] = far_prior[...] * keep
    left = rows_ref[:, :width]
    right = rows_ref[:, width:]
    prior = prior_ref[:width, :]
    gram_ref[:width, :] = dot(left, rows_ref[...], 0, 0) + dot(prior[:, :width], prior, 0, 0)
    corner = prior_ref[:, width:]
    gram_ref[width:, width:] = dot(right, right, 0, 0) + dot(corner, corner, 0, 0)
    gram_ref[width:, :width] = jnp.zeros((width, width), jnp.float32)


def panel_gram(count, spot, parts, near_prior, far_prior):
    slots = parts[0].shape[0] * 2 // count
    total, width = near_prior.shape
    return pl.pallas_call(
        functools.partial(panel_kernel, count),
        out_shape=(
            shape_of(count * slots, 2 * width),
            shape_of(total, 2 * width),
            shape_of(total, total),
        ),
        in_specs=[pl.BlockSpec(memory_space=pltpu.SMEM)] + [vmem_spec()] * 6,
        out_specs=(vmem_spec(),) * 3,
        compiler_params=params(),
        name="panel_gram",
    )(spot, *parts, near_prior, far_prior)


def info_kernel(plan, spot_ref, rows_ref, prior_panel_ref, *refs):
    count, slots, whole, halves = plan
    refs = list(refs)
    prior_whole = refs.pop(0) if whole else None
    prior_half = refs.pop(0)
    given = count if whole else count // 2
    pieces, out_ref = refs[:given], refs[given]
    half_rows = count // 2 * slots
    wide = whole * LANES
    if whole:
        work = refs[given + 1]
        for k in range(count):
            for b in range(whole):
                work[k * slots : (k + 1) * slots, b * LANES : (b + 1) * LANES] = pieces[k][
                    pl.ds(b, slots, stride=whole), :
                ]
        total = dot(rows_ref[...], work[...], 0, 0)
        flat = prior_whole.reshape(prior_whole.shape[0] * GROUP, LANES)
        for b in range(whole):
            work[: prior_whole.shape[0], b * LANES : (b + 1) * LANES] = flat[
                pl.ds(spot_ref[8] + b, prior_whole.shape[0], stride=GROUP), :
            ]
        out_ref[:, :wide] = total + dot(
            prior_panel_ref[...], work[: prior_whole.shape[0], :], 0, 0
        )
    work = refs[-1]
    own = prior_half.shape[0]
    for k in range(count // 2):
        for b in range(halves):
            work[k * slots : (k + 1) * slots, b * LANES : (b + 1) * LANES] = pieces[k][
                pl.ds(slots * whole + b, slots, stride=halves), :
            ]
    total = dot(rows_ref[:half_rows, :], work[:half_rows, :], 0, 0)
    flat = prior_half.reshape(own * GROUP, LANES)
    for b in range(halves):
        work[:own, b * LANES : (b + 1) * LANES] = flat[pl.ds(spot_ref[9] + b, own, stride=GROUP), :]
    panel = prior_panel_ref[pl.ds(pl.multiple_of(spot_ref[7] * own, own), own), :]
    out_ref[:, wide:] = total + dot(panel, work[:own, :], 0, 0)


def info_part(plan, spot, rows, prior_panel, prior, pieces):
    count, slots, whole, halves = plan
    total = prior.shape[0]
    full = lambda array: pl.BlockSpec(array.shape, lambda i, spot: (0,) * array.ndim)
    priors = [pl.BlockSpec((total // 2, None, GROUP, LANES), lambda i, spot: (spot[7], spot[6], 0, 0))]
    scratch = [pltpu.VMEM((count * slots // 2, halves * LANES), jnp.float32)]
    if whole:
        priors = [pl.BlockSpec((total, None, GROUP, LANES), lambda i, spot: (0, spot[5], 0, 0))] + priors
        scratch = [pltpu.VMEM((count * slots, whole * LANES), jnp.float32)] + scratch
    return pl.pallas_call(
        functools.partial(info_kernel, plan),
        out_shape=shape_of(total, (whole + halves) * LANES),
        grid_spec=pltpu.PrefetchScalarGridSpec(
            num_scalar_prefetch=1,
            grid=(1,),
            in_specs=[full(rows), full(prior_panel)] + priors + [full(piece) for piece in pieces],
            out_specs=pl.BlockSpec((total, (whole + halves) * LANES), lambda i, spot: (0, 0)),
            scratch_shapes=scratch,
        ),
        compiler_params=params(),
        name="info_part",
    )(spot, rows, prior_panel, *([prior] * len(priors)), *pieces)


def slab_kernel(plan, spot_ref, inverse_ref, own_ref, other_ref, out_ref):
    count, _, whole, halves = plan
    own_rows = inverse_ref.shape[0] // count
    blocks = whole + halves
    half = inverse_ref.shape[0] // 2
    tile = (own_rows, LANES)
    row_ids = lax.broadcasted_iota(jnp.int32, tile, 0)
    lane_ids = lax.broadcasted_iota(jnp.int32, tile, 1)
    info = own_ref[...] + other_ref[...]
    for side in range(2):
        depth = (side + 1) * half
        slab = dot(inverse_ref[side * half : depth, :depth], info[:depth, :], 1, 0)
        for b in range(blocks):
            for e in range(count // 2):
                d = side * (count // 2) + e
                part = slab[e * own_rows : (e + 1) * own_rows, b * LANES : (b + 1) * LANES]
                kept = jnp.where(spot_ref[SPOTS + b] + lane_ids >= row_ids + d * own_rows, part, 0.0)
                if b < whole:
                    at = pl.ds(b, own_rows, stride=whole)
                else:
                    at = pl.ds(own_rows * whole + b - whole, own_rows, stride=halves)
                out_ref[spot_ref[2] ^ d, at, :] = kept


def slab_part(plan, spot, inverse, own, other):
    count, _, whole, halves = plan
    total = own.shape[0]
    return pl.pallas_call(
        functools.partial(slab_kernel, plan),
        out_shape=shape_of(count, total // count * (whole + halves), LANES),
        in_specs=[pl.BlockSpec(memory_space=pltpu.SMEM)] + [vmem_spec()] * 3,
        out_specs=vmem_spec(),
        compiler_params=params(),
        name="slab_part",
    )(spot, inverse, own, other)


def place_kernel(plan, own_rows, spot_ref, *refs):
    count, _, whole, halves = plan
    parts, out_ref = refs[:count], refs[count]
    blocks = whole * count + halves * (count // 2)
    row = spot_ref[2]
    for k in range(count):
        for b in range(whole):
            at = pl.ds((row ^ k) * whole + b, own_rows, stride=blocks)
            out_ref[at, :] = parts[k][pl.ds(b, own_rows, stride=whole), :]
    for k in range(count // 2):
        pair = ((row ^ k) & (count // 2 - 1)) * halves + whole * count
        for b in range(halves):
            source = pl.ds(own_rows * whole + b, own_rows, stride=halves)
            total = parts[k][source, :] + parts[k + count // 2][source, :]
            out_ref[pl.ds(pair + b, own_rows, stride=blocks), :] = total


def place(plan, spot, parts):
    count, _, whole, halves = plan
    own_rows = parts[0].shape[0] // (whole + halves)
    blocks = whole * count + halves * (count // 2)
    return pl.pallas_call(
        functools.partial(place_kernel, plan, own_rows),
        out_shape=shape_of(own_rows * blocks, LANES),
        in_specs=[pl.BlockSpec(memory_space=pltpu.SMEM)] + [vmem_spec()] * count,
        out_specs=vmem_spec(),
        compiler_params=params(),
        name="place",
    )(spot, *parts)


def swapped(value, axis, bits):
    count = lax.axis_size(axis)
    return lax.ppermute(value, axis, [(i, i ^ bits) for i in range(count)])


def handed_on(value):
    return lax.ppermute(value, "section", [(0, 1)])


def panels_of(near, near_prior):
    rows, cols = lax.axis_size("row"), lax.axis_size("col")
    far_prior = swapped(near_prior, "col", 1) if cols == 2 else None
    near = jnp.concatenate([near] + [swapped(near, "row", k) for k in range(2, rows, 2)], axis=0)
    if cols == 2:
        order = [(i, i ^ 3) for i in range(rows * cols)]
        far = [swapped(near, "col", 1), lax.ppermute(near, ("row", "col"), order)]
        return [near, swapped(near, "row", 1)] + far, near_prior, far_prior
    priors = lax.all_gather(near_prior, "col")
    both = lax.all_gather(near, "col")
    both = [both[0], both[1]]
    beside = [swapped(panel, "row", 1) for panel in both]
    return [both[0], beside[0], both[1], beside[1]], priors[0], priors[1]


def on_device(prior_root, observations, live_rows):
    total, cycles, _, width = prior_root.shape
    slots = observations.shape[1]
    rows, cols = lax.axis_size("row"), lax.axis_size("col")
    half = rows // 2
    per = width // LANES
    blocks = cycles * per
    whole = blocks // (2 * rows)
    halves = (blocks - rows * whole) // half
    plan = (rows, slots, whole, halves)
    col, row, section = (lax.axis_index(axis) for axis in ("col", "row", "section"))
    first = row * whole
    first_half = rows * whole + row % half * halves
    mine = [first + b for b in range(whole)] + [first_half + b for b in range(halves)]
    spot = [
        col if cols == 2 else 0,
        section,
        row,
        0,
        0,
        first // GROUP,
        first_half // GROUP,
        row // half,
        first % GROUP,
        first_half % GROUP,
    ]
    spot += [(j // per * cols + col) * width + j % per * LANES for j in mine]
    spot = jnp.stack([jnp.asarray(value, jnp.int32) for value in spot])
    prior = prior_root.reshape(total, blocks // GROUP, GROUP, LANES)
    live = lax.broadcasted_iota(jnp.int32, (slots, 1), 0) < live_rows[0, 0]
    near = jnp.where(live, observations[0, :, 0, 0, :], 0.0)
    parts, near_prior, far_prior = panels_of(near, prior_root[:, 0, 0, :])
    observed = observations.reshape(slots, blocks, LANES)
    of_whole = observed[:, : rows * whole].reshape(slots, rows, whole, LANES)
    of_half = observed[:, rows * whole :].reshape(slots, half, halves, LANES)
    pieces = [None] * rows
    for k in list(range(half, rows)) + list(range(half)):
        chosen = []
        if whole:
            piece = lax.dynamic_index_in_dim(of_whole, row ^ k, 1, keepdims=False)
            chosen.append(piece.reshape(slots * whole, LANES))
        if k < half:
            piece = lax.dynamic_index_in_dim(of_half, (row ^ k) % half, 1, keepdims=False)
            chosen.append(piece.reshape(slots * halves, LANES))
        if chosen:
            piece = jnp.concatenate(chosen, axis=0)
            pieces[k] = swapped(piece, "row", k) if k else piece
    pieces = [piece for piece in pieces if piece is not None]
    rows_panel, prior_panel, gram = panel_gram(rows, spot, parts, near_prior, far_prior)
    inverse = factor(gram, handed_on(gram))
    info = info_part(plan, spot, rows_panel, prior_panel, prior, pieces)
    slab = slab_part(plan, spot, inverse, info, handed_on(info))
    parts = [None] * rows
    for k in list(range(half, rows)) + list(range(half)):
        parts[k] = swapped(slab[k], "row", k) if k else slab[0]
    out = place(plan, spot, parts)
    return out.reshape(1, total // rows, cycles, 1, width)


def solution(mesh):
    placed = (
        P(None, None, "col", None),
        P("section", "row", None, "col", None),
        P("section", "row"),
    )
    return jax.shard_map(
        on_device,
        mesh=mesh,
        in_specs=placed,
        out_specs=P("section", "row", None, "col", None),
        check_vma=False,
    )
```

```python
import functools

import jax
import jax.numpy as jnp
from jax import lax
from jax.experimental import pallas as pl
from jax.experimental.pallas import tpu as pltpu
from jax.sharding import PartitionSpec as P

LANES = 128
TALL = 16
GROUP = 8
SPOTS = 6
VMEM_BYTES = 56 * 2**20


def dot(left, right, contract_left, contract_right):
    return lax.dot_general(
        left,
        right,
        (((contract_left,), (contract_right,)), ((), ())),
        precision=lax.Precision.HIGHEST,
        preferred_element_type=jnp.float32,
    )


def spread(row, shape):
    return jnp.broadcast_to(row, shape)


def factor_block(work_ref):
    size = work_ref.shape[0]
    tile = (8, LANES)
    row_ids = lax.broadcasted_iota(jnp.int32, tile, 0)
    for first in range(0, size, TALL):
        middle, end = first + 8, first + TALL
        top = [work_ref[first:middle, t * LANES : (t + 1) * LANES] for t in range(2)]
        low = [work_ref[middle:end, t * LANES : (t + 1) * LANES] for t in range(2)]
        top_col = [spread(top[0][:, first + k : first + k + 1], tile) for k in range(TALL)]
        low_col = [spread(low[0][:, first + k : first + k + 1], tile) for k in range(TALL)]
        top_pivot = jnp.ones(tile, jnp.float32)
        low_pivot = jnp.ones(tile, jnp.float32)
        for step in range(TALL):
            if step < 8:
                pivot = spread(top_col[step][step : step + 1], tile)
                inverse = 1.0 / pivot
                top_by = jnp.where(row_ids > step, top_col[step] * inverse, 0.0)
                low_by = low_col[step] * inverse
                top_pivot = jnp.where(row_ids == step, pivot, top_pivot)
                for k in range(step + 1, TALL):
                    lead = spread(top_col[k][step : step + 1], tile)
                    top_col[k] = top_col[k] - top_by * lead
                    low_col[k] = low_col[k] - low_by * lead
                for t in range(2):
                    lead = spread(top[t][step : step + 1], tile)
                    top[t] = top[t] - top_by * lead
                    low[t] = low[t] - low_by * lead
            else:
                at = step - 8
                pivot = spread(low_col[step][at : at + 1], tile)
                low_by = jnp.where(row_ids > at, low_col[step] * (1.0 / pivot), 0.0)
                low_pivot = jnp.where(row_ids == at, pivot, low_pivot)
                for k in range(step + 1, TALL):
                    low_col[k] = low_col[k] - low_by * spread(low_col[k][at : at + 1], tile)
                for t in range(2):
                    low[t] = low[t] - low_by * spread(low[t][at : at + 1], tile)
        top_scale, low_scale = lax.rsqrt(top_pivot), lax.rsqrt(low_pivot)
        for t in range(2):
            work_ref[first:middle, t * LANES : (t + 1) * LANES] = top[t] * top_scale
            work_ref[middle:end, t * LANES : (t + 1) * LANES] = low[t] * low_scale
        if end < size:
            done = work_ref[first:end, :]
            change = dot(done[:, :LANES], done, 0, 0)
            work_ref[end:, :] = work_ref[end:, :] - change[end:, :]


def factor_kernel(own_ref, other_ref, inverse_ref, info_ref, work_ref):
    size = own_ref.shape[0]
    ids = [lax.broadcasted_iota(jnp.int32, (LANES, LANES), axis) for axis in range(2)]
    eye = (ids[0] == ids[1]).astype(jnp.float32)
    info_ref[...] = own_ref[...] + other_ref[...]
    inverse_ref[...] = jnp.zeros_like(inverse_ref)
    for start in range(0, size, LANES):
        end = start + LANES
        work_ref[:, :LANES] = info_ref[start:end, start:end]
        work_ref[:, LANES:] = eye
        factor_block(work_ref)
        block = work_ref[:, LANES:]
        if start:
            inverse_ref[start:end, :start] = dot(block, inverse_ref[start:end, :start], 1, 0)
        inverse_ref[start:end, start:end] = block
        if end < size:
            upper = dot(block, info_ref[start:end, end:], 1, 0)
            info_ref[end:, end:] = info_ref[end:, end:] - dot(upper, upper, 0, 0)
            inverse_ref[end:, :end] = inverse_ref[end:, :end] - dot(
                upper, inverse_ref[start:end, :end], 0, 0
            )


def vmem_spec():
    return pl.BlockSpec(memory_space=pltpu.VMEM)


def params():
    return pltpu.CompilerParams(vmem_limit_bytes=VMEM_BYTES)


def shape_of(*shape):
    return jax.ShapeDtypeStruct(shape, jnp.float32)


def factor(own, other):
    size = own.shape[0]
    return pl.pallas_call(
        factor_kernel,
        out_shape=shape_of(size, size),
        in_specs=[vmem_spec()] * 2,
        out_specs=vmem_spec(),
        scratch_shapes=[
            pltpu.VMEM((size, size), jnp.float32),
            pltpu.VMEM((LANES, 2 * LANES), jnp.float32),
        ],
        compiler_params=params(),
        name="factor",
    )(own, other)


def panel_kernel(count, spot_ref, near_ref, *refs):
    near_prior, far_prior, rows_ref, prior_ref, gram_ref = refs[-5:]
    parts = refs[:-5]
    width = near_prior.shape[1]
    col, section = spot_ref[0], spot_ref[1]
    near_at = pl.ds(pl.multiple_of(col * width, width), width)
    far_at = pl.ds(pl.multiple_of((1 - col) * width, width), width)
    slots = near_ref.shape[0] * 2 // count
    near_next, far_here, far_next = parts
    pair = spot_ref[2] // 2
    for i in range(count // 2):
        here, beside = (pl.ds(((pair ^ i) + side) * slots, slots) for side in (0, count // 2))
        piece = slice(i * slots, (i + 1) * slots)
        rows_ref[here, near_at] = near_ref[piece]
        rows_ref[beside, near_at] = near_next[piece]
        rows_ref[here, far_at] = far_here[piece]
        rows_ref[beside, far_at] = far_next[piece]
    keep = (section == 0).astype(jnp.float32)
    prior_ref[:, near_at] = near_prior[...] * keep
    prior_ref[:, far_at] = far_prior[...] * keep
    left = rows_ref[:, :width]
    right = rows_ref[:, width:]
    prior = prior_ref[:width, :]
    gram_ref[:width, :] = dot(left, rows_ref[...], 0, 0) + dot(prior[:, :width], prior, 0, 0)
    corner = prior_ref[:, width:]
    gram_ref[width:, width:] = dot(right, right, 0, 0) + dot(corner, corner, 0, 0)
    gram_ref[width:, :width] = jnp.zeros((width, width), jnp.float32)


def panel_gram(count, spot, parts, near_prior, far_prior):
    slots = parts[0].shape[0] * 2 // count
    total, width = near_prior.shape
    return pl.pallas_call(
        functools.partial(panel_kernel, count),
        out_shape=(
            shape_of(count * slots, 2 * width),
            shape_of(total, 2 * width),
            shape_of(total, total),
        ),
        in_specs=[pl.BlockSpec(memory_space=pltpu.SMEM)] + [vmem_spec()] * 6,
        out_specs=(vmem_spec(),) * 3,
        compiler_params=params(),
        name="panel_gram",
    )(spot, *parts, near_prior, far_prior)


def gather_blocks(ref, first, rows, stride, blocks, work, at):
    for b in range(blocks):
        work[at : at + rows, b * LANES : (b + 1) * LANES] = ref[pl.ds(first + b, rows, stride=stride), :]


def pack_kernel(sizes, spot_ref, observed_ref, far_ref, *own_refs):
    slots, blocks, pairs, chunk, parts = sizes
    each = chunk // parts
    side = spot_ref[2] & 1
    for part in range(parts):
        for pair in range(pairs):
            for b in range(each):
                here = (2 * pair + side) * chunk + part * each + b
                there = (2 * pair + 1 - side) * chunk + part * each + b
                at = pl.ds(b, slots, stride=each)
                own_refs[part][pair, at, :] = observed_ref[pl.ds(here, slots, stride=blocks), :]
                far_ref[pair, part, at, :] = observed_ref[pl.ds(there, slots, stride=blocks), :]


def pack(sizes, spot, observed):
    slots, _, pairs, chunk, parts = sizes
    size = slots * chunk // parts
    return pl.pallas_call(
        functools.partial(pack_kernel, sizes),
        out_shape=(shape_of(pairs, parts, size, LANES),) + (shape_of(pairs, size, LANES),) * parts,
        in_specs=[pl.BlockSpec(memory_space=pltpu.SMEM), vmem_spec()],
        out_specs=(vmem_spec(),) * (1 + parts),
        compiler_params=params(),
        name="pack",
    )(spot, observed)


def info_kernel(each, spot_ref, rows_ref, panel_ref, prior_ref, near_ref, far_ref, out_ref, work):
    total, group = prior_ref.shape[0], prior_ref.shape[1]
    count = rows_ref.shape[0]
    flat = prior_ref.reshape(total * group, LANES)
    gather_blocks(flat, spot_ref[5], total, group, each, work, 0)
    part = dot(panel_ref[...], work[:total, :], 0, 0)
    gather_blocks(near_ref, 0, count // 2, each, each, work, 0)
    gather_blocks(far_ref, 0, count // 2, each, each, work, count // 2)
    out_ref[...] = part + dot(rows_ref[...], work[:count, :], 0, 0)


def info_part(each, spot, rows, panel, prior, near, far):
    total, _, group, _ = prior.shape
    full = lambda array: pl.BlockSpec(array.shape, lambda i, spot: (0,) * array.ndim)
    return pl.pallas_call(
        functools.partial(info_kernel, each),
        out_shape=shape_of(total, each * LANES),
        grid_spec=pltpu.PrefetchScalarGridSpec(
            num_scalar_prefetch=1,
            grid=(1,),
            in_specs=[
                full(rows),
                full(panel),
                pl.BlockSpec((total, None, group, LANES), lambda i, spot: (0, spot[4], 0, 0)),
                full(near),
                full(far),
            ],
            out_specs=pl.BlockSpec((total, each * LANES), lambda i, spot: (0, 0)),
            scratch_shapes=[pltpu.VMEM((max(total, rows.shape[0]), each * LANES), jnp.float32)],
        ),
        compiler_params=params(),
        name="info_part",
    )(spot, rows, panel, prior, near, far)


def slab_kernel(count, spot_ref, inverse_ref, own_ref, other_ref, out_ref):
    total, width = own_ref.shape
    own_rows, chunk = total // count, width // LANES
    half = total // 2
    tile = (own_rows, LANES)
    row_ids = lax.broadcasted_iota(jnp.int32, tile, 0)
    lane_ids = lax.broadcasted_iota(jnp.int32, tile, 1)
    info = own_ref[...] + other_ref[...]
    for side in range(2):
        depth = (side + 1) * half
        slab = dot(inverse_ref[side * half : depth, :depth], info[:depth, :], 1, 0)
        for b in range(chunk):
            for e in range(count // 2):
                d = side * (count // 2) + e
                part = slab[e * own_rows : (e + 1) * own_rows, b * LANES : (b + 1) * LANES]
                kept = jnp.where(spot_ref[SPOTS + b] + lane_ids >= row_ids + d * own_rows, part, 0.0)
                out_ref[d, pl.ds(b, own_rows, stride=chunk), :] = kept


def slab_part(count, spot, inverse, own, other):
    total, width = own.shape
    return pl.pallas_call(
        functools.partial(slab_kernel, count),
        out_shape=shape_of(count, total // count * width // LANES, LANES),
        in_specs=[pl.BlockSpec(memory_space=pltpu.SMEM)] + [vmem_spec()] * 3,
        out_specs=vmem_spec(),
        compiler_params=params(),
        name="slab_part",
    )(spot, inverse, own, other)


def swapped(value, axis, bits):
    count = lax.axis_size(axis)
    return lax.ppermute(value, axis, [(i, i ^ bits) for i in range(count)])


def handed_on(value):
    return lax.ppermute(value, "section", [(0, 1)])


def panels_of(near, near_prior):
    rows, cols = lax.axis_size("row"), lax.axis_size("col")
    far_prior = swapped(near_prior, "col", 1) if cols == 2 else None
    near = jnp.concatenate([near] + [swapped(near, "row", k) for k in range(2, rows, 2)], axis=0)
    if cols == 2:
        order = [(i, i ^ 3) for i in range(rows * cols)]
        far = [swapped(near, "col", 1), lax.ppermute(near, ("row", "col"), order)]
        return [near, swapped(near, "row", 1)] + far, near_prior, far_prior, near
    priors = lax.all_gather(near_prior, "col")
    both = lax.all_gather(near, "col")
    both = [both[0], both[1]]
    beside = [swapped(panel, "row", 1) for panel in both]
    return [both[0], beside[0], both[1], beside[1]], priors[0], priors[1], near


def on_device(prior_root, observations, live_rows):
    total, cycles, _, width = prior_root.shape
    slots = observations.shape[1]
    rows, cols = lax.axis_size("row"), lax.axis_size("col")
    per = width // LANES
    blocks = cycles * per
    chunk = -(-blocks // rows)
    parts = 2 if chunk % 2 == 0 else 1
    each = chunk // parts
    col, row, section = (lax.axis_index(axis) for axis in ("col", "row", "section"))
    group = min(GROUP, chunk * rows)

    def spot_of(part):
        first = row * chunk + part * each
        spot = [col if cols == 2 else 0, section, row, 0, first // group, first % group]
        spot += [((first + b) // per * cols + col) * width + (first + b) % per * LANES for b in range(each)]
        return jnp.stack([jnp.asarray(value, jnp.int32) for value in spot])

    def in_blocks(array):
        array = array.reshape(array.shape[0], blocks, LANES)
        return jnp.pad(array, ((0, 0), (0, chunk * rows - blocks), (0, 0)))

    spots = [spot_of(part) for part in range(parts)]
    prior = in_blocks(prior_root.reshape(total, -1)).reshape(total, -1, group, LANES)
    observed = in_blocks(observations.reshape(slots, -1)).reshape(-1, LANES)
    live = lax.broadcasted_iota(jnp.int32, (slots, 1), 0) < live_rows[0, 0]
    near = jnp.where(live, observations[0, :, 0, 0, :], 0.0)
    panels, near_prior, far_prior, near = panels_of(near, prior_root[:, 0, 0, :])
    far, *own = pack((slots, chunk * rows, rows // 2, chunk, parts), spots[0], observed)
    same_side = [[2 * i + side for i in range(rows // 2)] for side in range(2)]

    def over(piece):
        return lax.all_to_all(piece, "row", 0, 0, axis_index_groups=same_side, tiled=True)

    far, near = lax.optimization_barrier((far, near))
    far = over(far)
    far = [far[:, part].reshape(-1, LANES) for part in range(parts)]
    far, _ = lax.optimization_barrier((far, panels))
    far = [swapped(piece, "row", 1) for piece in far]
    rows_panel, prior_panel, gram = panel_gram(rows, spots[0], panels, near_prior, far_prior)
    other_gram = handed_on(gram)
    own[0], gram, other_gram = lax.optimization_barrier((own[0], gram, other_gram))
    inverse = factor(gram, other_gram)
    slabs, last = [], None
    for part in range(parts):
        if part:
            own[part], inverse, last = lax.optimization_barrier((own[part], inverse, last))
        last = over(own[part])
        near_rows = last.reshape(-1, LANES)
        info = info_part(each, spots[part], rows_panel, prior_panel, prior, near_rows, far[part])
        other = handed_on(info)
        if part + 1 < parts:
            other, far[part + 1] = lax.optimization_barrier((other, far[part + 1]))
        slab = slab_part(rows, spots[part], inverse, info, other)
        slab = lax.all_to_all(slab, "row", 0, 0, tiled=True)
        slabs.append(slab.reshape(rows, total // rows, each, LANES))
    out = jnp.stack(slabs, axis=2).reshape(rows, total // rows, chunk, LANES).transpose(1, 0, 2, 3)
    out = out.reshape(total // rows, rows * chunk, LANES)[:, :blocks]
    return out.reshape(1, total // rows, cycles, 1, width)


def solution(mesh):
    placed = (
        P(None, None, "col", None),
        P("section", "row", None, "col", None),
        P("section", "row"),
    )
    return jax.shard_map(
        on_device,
        mesh=mesh,
        in_specs=placed,
        out_specs=P("section", "row", None, "col", None),
        check_vma=False,
    )
```

```python
import functools

import jax
import jax.numpy as jnp
from jax import lax
from jax.experimental import pallas as pl
from jax.experimental.pallas import tpu as pltpu
from jax.sharding import PartitionSpec as P

LANES = 128
TALL = 16
GROUP = 8
SPOTS = 6
VMEM_BYTES = 56 * 2**20


def dot(left, right, contract_left, contract_right):
    return lax.dot_general(
        left,
        right,
        (((contract_left,), (contract_right,)), ((), ())),
        precision=lax.Precision.HIGHEST,
        preferred_element_type=jnp.float32,
    )


def thirds(value):
    high = value.astype(jnp.bfloat16)
    rest = value - high.astype(jnp.float32)
    middle = rest.astype(jnp.bfloat16)
    return high, middle, (rest - middle.astype(jnp.float32)).astype(jnp.bfloat16)


def short_dot(left, right, contract_left, contract_right):
    a, b = thirds(left), thirds(right)
    left = jnp.concatenate([a[0], a[0], a[1], a[1], a[0], a[2]], axis=contract_left)
    right = jnp.concatenate([b[0], b[1], b[0], b[1], b[2], b[0]], axis=contract_right)
    return lax.dot_general(
        left,
        right,
        (((contract_left,), (contract_right,)), ((), ())),
        preferred_element_type=jnp.float32,
    )


def spread(row, shape):
    return jnp.broadcast_to(row, shape)


def factor_block(work_ref):
    size = work_ref.shape[0]
    tile = (8, LANES)
    row_ids = lax.broadcasted_iota(jnp.int32, tile, 0)
    for first in range(0, size, TALL):
        middle, end = first + 8, first + TALL
        top = [work_ref[first:middle, t * LANES : (t + 1) * LANES] for t in range(2)]
        low = [work_ref[middle:end, t * LANES : (t + 1) * LANES] for t in range(2)]
        top_col = [spread(top[0][:, first + k : first + k + 1], tile) for k in range(TALL)]
        low_col = [spread(low[0][:, first + k : first + k + 1], tile) for k in range(TALL)]
        top_pivot = jnp.ones(tile, jnp.float32)
        low_pivot = jnp.ones(tile, jnp.float32)
        for step in range(TALL):
            if step < 8:
                pivot = spread(top_col[step][step : step + 1], tile)
                inverse = 1.0 / pivot
                top_by = jnp.where(row_ids > step, top_col[step] * inverse, 0.0)
                low_by = low_col[step] * inverse
                top_pivot = jnp.where(row_ids == step, pivot, top_pivot)
                for k in range(step + 1, TALL):
                    lead = spread(top_col[k][step : step + 1], tile)
                    top_col[k] = top_col[k] - top_by * lead
                    low_col[k] = low_col[k] - low_by * lead
                for t in range(2):
                    lead = spread(top[t][step : step + 1], tile)
                    top[t] = top[t] - top_by * lead
                    low[t] = low[t] - low_by * lead
            else:
                at = step - 8
                pivot = spread(low_col[step][at : at + 1], tile)
                low_by = jnp.where(row_ids > at, low_col[step] * (1.0 / pivot), 0.0)
                low_pivot = jnp.where(row_ids == at, pivot, low_pivot)
                for k in range(step + 1, TALL):
                    low_col[k] = low_col[k] - low_by * spread(low_col[k][at : at + 1], tile)
                for t in range(2):
                    low[t] = low[t] - low_by * spread(low[t][at : at + 1], tile)
        top_scale, low_scale = lax.rsqrt(top_pivot), lax.rsqrt(low_pivot)
        for t in range(2):
            work_ref[first:middle, t * LANES : (t + 1) * LANES] = top[t] * top_scale
            work_ref[middle:end, t * LANES : (t + 1) * LANES] = low[t] * low_scale
        if end < size:
            done = work_ref[first:end, :]
            change = short_dot(done[:, :LANES], done, 0, 0)
            work_ref[end:, :] = work_ref[end:, :] - change[end:, :]


def factor_kernel(own_ref, other_ref, inverse_ref, info_ref, work_ref):
    size = own_ref.shape[0]
    ids = [lax.broadcasted_iota(jnp.int32, (LANES, LANES), axis) for axis in range(2)]
    eye = (ids[0] == ids[1]).astype(jnp.float32)
    info_ref[...] = own_ref[...] + other_ref[...]
    inverse_ref[...] = jnp.zeros_like(inverse_ref)
    for start in range(0, size, LANES):
        end = start + LANES
        work_ref[:, :LANES] = info_ref[start:end, start:end]
        work_ref[:, LANES:] = eye
        factor_block(work_ref)
        block = work_ref[:, LANES:]
        if start:
            inverse_ref[start:end, :start] = short_dot(block, inverse_ref[start:end, :start], 1, 0)
        inverse_ref[start:end, start:end] = block
        if end < size:
            upper = short_dot(block, info_ref[start:end, end:], 1, 0)
            info_ref[end:, end:] = info_ref[end:, end:] - short_dot(upper, upper, 0, 0)
            inverse_ref[end:, :end] = inverse_ref[end:, :end] - short_dot(
                upper, inverse_ref[start:end, :end], 0, 0
            )


def vmem_spec():
    return pl.BlockSpec(memory_space=pltpu.VMEM)


def params():
    return pltpu.CompilerParams(vmem_limit_bytes=VMEM_BYTES)


def shape_of(*shape):
    return jax.ShapeDtypeStruct(shape, jnp.float32)


def factor(own, other):
    size = own.shape[0]
    return pl.pallas_call(
        factor_kernel,
        out_shape=shape_of(size, size),
        in_specs=[vmem_spec()] * 2,
        out_specs=vmem_spec(),
        scratch_shapes=[
            pltpu.VMEM((size, size), jnp.float32),
            pltpu.VMEM((LANES, 2 * LANES), jnp.float32),
        ],
        compiler_params=params(),
        name="factor",
    )(own, other)


def panel_kernel(count, spot_ref, near_ref, *refs):
    near_prior, far_prior, rows_ref, prior_ref, gram_ref = refs[-5:]
    parts = refs[:-5]
    width = near_prior.shape[1]
    col, section = spot_ref[0], spot_ref[1]
    near_at = pl.ds(pl.multiple_of(col * width, width), width)
    far_at = pl.ds(pl.multiple_of((1 - col) * width, width), width)
    slots = near_ref.shape[0] * 2 // count
    near_next, far_here, far_next = parts
    pair = spot_ref[2] // 2
    for i in range(count // 2):
        here, beside = (pl.ds(((pair ^ i) + side) * slots, slots) for side in (0, count // 2))
        piece = slice(i * slots, (i + 1) * slots)
        rows_ref[here, near_at] = near_ref[piece]
        rows_ref[beside, near_at] = near_next[piece]
        rows_ref[here, far_at] = far_here[piece]
        rows_ref[beside, far_at] = far_next[piece]
    keep = (section == 0).astype(jnp.float32)
    prior_ref[:, near_at] = near_prior[...] * keep
    prior_ref[:, far_at] = far_prior[...] * keep
    left = rows_ref[:, :width]
    right = rows_ref[:, width:]
    prior = prior_ref[:width, :]
    gram_ref[:width, :] = dot(left, rows_ref[...], 0, 0) + dot(prior[:, :width], prior, 0, 0)
    corner = prior_ref[:, width:]
    gram_ref[width:, width:] = dot(right, right, 0, 0) + dot(corner, corner, 0, 0)
    gram_ref[width:, :width] = jnp.zeros((width, width), jnp.float32)


def panel_gram(count, spot, parts, near_prior, far_prior):
    slots = parts[0].shape[0] * 2 // count
    total, width = near_prior.shape
    return pl.pallas_call(
        functools.partial(panel_kernel, count),
        out_shape=(
            shape_of(count * slots, 2 * width),
            shape_of(total, 2 * width),
            shape_of(total, total),
        ),
        in_specs=[pl.BlockSpec(memory_space=pltpu.SMEM)] + [vmem_spec()] * 6,
        out_specs=(vmem_spec(),) * 3,
        compiler_params=params(),
        name="panel_gram",
    )(spot, *parts, near_prior, far_prior)


def gather_blocks(ref, first, rows, stride, blocks, work, at):
    for b in range(blocks):
        work[at : at + rows, b * LANES : (b + 1) * LANES] = ref[pl.ds(first + b, rows, stride=stride), :]


def pack_kernel(first, each, joined, spot_ref, *refs):
    *sources, out_ref = refs
    outs = [out_ref] if len(out_ref.shape) == 2 else [out_ref.at[i] for i in range(2)]
    if joined:
        outs.pop(0)[...] = sources.pop(0)[...]
    for source, out in zip(sources, outs):
        slots, chunk, _ = source.shape
        flat = source.reshape(slots * chunk, LANES)
        for b in range(each):
            out[pl.ds(b, slots, stride=each), :] = flat[pl.ds(first + b, slots, stride=chunk), :]


def pack(spot, observed, part, each, sides, swapped_blocks=None):
    slots, rows, chunk, _ = observed.shape
    size = slots * each

    def source(side):
        at = lambda i, spot: (0, 2 * i + (spot[2] + side) % 2, 0, 0)
        return pl.BlockSpec((slots, None, chunk, LANES), at)

    specs, arrays = [source(side) for side in sides], [observed] * len(sides)
    if swapped_blocks is not None:
        specs = [pl.BlockSpec((None, size, LANES), lambda i, spot: (i, 0, 0))] + specs
        arrays = [swapped_blocks] + arrays
    if len(specs) == 1:
        out, out_spec = (rows // 2, size), pl.BlockSpec((None, size, LANES), lambda i, spot: (i, 0, 0))
    else:
        out = (rows // 2, 2, size)
        out_spec = pl.BlockSpec((None, 2, size, LANES), lambda i, spot: (i, 0, 0, 0))
    return pl.pallas_call(
        functools.partial(pack_kernel, part * each, each, swapped_blocks is not None),
        out_shape=shape_of(*out, LANES),
        grid_spec=pltpu.PrefetchScalarGridSpec(
            num_scalar_prefetch=1, grid=(rows // 2,), in_specs=specs, out_specs=out_spec
        ),
        compiler_params=params(),
        name="pack",
    )(spot, *arrays)


def plain_pack(spot, observed):
    slots, rows, chunk, _ = observed.shape
    pairs = observed.reshape(slots, rows // 2, 2, chunk, LANES).transpose(1, 2, 0, 3, 4)
    sides = [lax.dynamic_index_in_dim(pairs, (spot[2] + side) % 2, 1, keepdims=False) for side in (1, 0)]
    return jnp.stack(sides, axis=1).reshape(rows // 2, 2, slots * chunk, LANES)


def info_kernel(each, spot_ref, rows_ref, panel_ref, prior_ref, far_ref, near_ref, out_ref, work):
    total, group = prior_ref.shape[0], prior_ref.shape[1]
    count, pairs = rows_ref.shape[0], far_ref.shape[0]
    slots = count // 2 // pairs
    flat = prior_ref.reshape(total * group, LANES)
    gather_blocks(flat, spot_ref[5], total, group, each, work, 0)
    part = dot(panel_ref[...], work[:total, :], 0, 0)
    for i in range(pairs):
        gather_blocks(near_ref.at[i], 0, slots, each, each, work, i * slots)
        gather_blocks(far_ref.at[i], 0, slots, each, each, work, count // 2 + i * slots)
    out_ref[...] = part + dot(rows_ref[...], work[:count, :], 0, 0)


def info_part(each, spot, rows, panel, prior, far, near):
    total, _, group, _ = prior.shape
    full = lambda array: pl.BlockSpec(array.shape, lambda i, spot: (0,) * array.ndim)
    half = lambda array, at: pl.BlockSpec(
        (array.shape[0], None) + array.shape[2:], lambda i, spot: (0, at, 0, 0)
    )
    return pl.pallas_call(
        functools.partial(info_kernel, each),
        out_shape=shape_of(total, each * LANES),
        grid_spec=pltpu.PrefetchScalarGridSpec(
            num_scalar_prefetch=1,
            grid=(1,),
            in_specs=[
                full(rows),
                full(panel),
                pl.BlockSpec((total, None, group, LANES), lambda i, spot: (0, spot[4], 0, 0)),
                full(far) if far.ndim == 3 else half(far, 0),
                half(near, 1),
            ],
            out_specs=pl.BlockSpec((total, each * LANES), lambda i, spot: (0, 0)),
            scratch_shapes=[pltpu.VMEM((max(total, rows.shape[0]), each * LANES), jnp.float32)],
        ),
        compiler_params=params(),
        name="info_part",
    )(spot, rows, panel, prior, far, near)


def slab_kernel(count, spot_ref, inverse_ref, own_ref, other_ref, out_ref):
    total, width = own_ref.shape
    own_rows, chunk = total // count, width // LANES
    half = total // 2
    tile = (own_rows, LANES)
    row_ids = lax.broadcasted_iota(jnp.int32, tile, 0)
    lane_ids = lax.broadcasted_iota(jnp.int32, tile, 1)
    info = own_ref[...] + other_ref[...]
    for side in range(2):
        depth = (side + 1) * half
        slab = dot(inverse_ref[side * half : depth, :depth], info[:depth, :], 1, 0)
        for b in range(chunk):
            for e in range(count // 2):
                d = side * (count // 2) + e
                part = slab[e * own_rows : (e + 1) * own_rows, b * LANES : (b + 1) * LANES]
                kept = jnp.where(spot_ref[SPOTS + b] + lane_ids >= row_ids + d * own_rows, part, 0.0)
                out_ref[d, pl.ds(b, own_rows, stride=chunk), :] = kept


def slab_part(count, spot, inverse, own, other):
    total, width = own.shape
    return pl.pallas_call(
        functools.partial(slab_kernel, count),
        out_shape=shape_of(count, total // count * width // LANES, LANES),
        in_specs=[pl.BlockSpec(memory_space=pltpu.SMEM)] + [vmem_spec()] * 3,
        out_specs=vmem_spec(),
        compiler_params=params(),
        name="slab_part",
    )(spot, inverse, own, other)


def swapped(value, axis, bits):
    count = lax.axis_size(axis)
    return lax.ppermute(value, axis, [(i, i ^ bits) for i in range(count)])


def handed_on(value):
    return lax.ppermute(value, "section", [(0, 1)])


def z_panels(near):
    rows = lax.axis_size("row")
    return jnp.concatenate([near] + [swapped(near, "row", k) for k in range(2, rows, 2)], axis=0)


def prior_panels(near_prior):
    if lax.axis_size("col") == 2:
        return near_prior, swapped(near_prior, "col", 1)
    priors = lax.all_gather(near_prior, "col")
    return priors[0], priors[1]


def all_panels(near):
    rows, cols = lax.axis_size("row"), lax.axis_size("col")
    if cols == 2:
        order = [(i, i ^ 3) for i in range(rows * cols)]
        far = [swapped(near, "col", 1), lax.ppermute(near, ("row", "col"), order)]
        return [near, swapped(near, "row", 1)] + far
    both = lax.all_gather(near, "col")
    both = [both[0], both[1]]
    beside = [swapped(panel, "row", 1) for panel in both]
    return [both[0], beside[0], both[1], beside[1]]


def on_device(prior_root, observations, live_rows):
    total, cycles, _, width = prior_root.shape
    slots = observations.shape[1]
    rows, cols = lax.axis_size("row"), lax.axis_size("col")
    per = width // LANES
    blocks = cycles * per
    chunk = -(-blocks // rows)
    parts = 2 if chunk % GROUP == 0 else 1
    each = chunk // parts
    col, row, section = (lax.axis_index(axis) for axis in ("col", "row", "section"))
    group = min(GROUP, chunk * rows)

    def spot_of(part):
        first = row * chunk + part * each
        spot = [col if cols == 2 else 0, section, row, 0, first // group, first % group]
        spot += [((first + b) // per * cols + col) * width + (first + b) % per * LANES for b in range(each)]
        return jnp.stack([jnp.asarray(value, jnp.int32) for value in spot])

    def in_blocks(array):
        array = array.reshape(array.shape[0], blocks, LANES)
        return jnp.pad(array, ((0, 0), (0, chunk * rows - blocks), (0, 0)))

    spots = [spot_of(part) for part in range(parts)]
    prior = in_blocks(prior_root.reshape(total, -1)).reshape(total, -1, group, LANES)
    observed = in_blocks(observations.reshape(slots, -1)).reshape(slots, rows, chunk, LANES)
    live = lax.broadcasted_iota(jnp.int32, (slots, 1), 0) < live_rows[0, 0]
    near = jnp.where(live, observations[0, :, 0, 0, :], 0.0)
    same_side = [[2 * i + side for i in range(rows // 2)] for side in range(2)]

    def over(piece):
        return lax.all_to_all(piece, "row", 0, 0, axis_index_groups=same_side, tiled=True)

    near = z_panels(near)
    if parts > 1:
        crossing = pack(spots[0], observed, 1, each, [1])
        packed = pack(spots[0], observed, 0, each, [1, 0])
        packed, crossing, near = lax.optimization_barrier((packed, crossing, near))
        crossed = swapped(crossing, "row", 1)
    else:
        packed, near = lax.optimization_barrier((plain_pack(spots[0], observed), near))
    priors = prior_panels(prior_root[:, 0, 0, :])
    near, priors = lax.optimization_barrier((near, priors))
    panels = all_panels(near)
    first = over(packed)
    far = first[:, 0]
    far, _ = lax.optimization_barrier((far, panels))
    arrived = [(swapped(far, "row", 1), first)]
    if parts > 1:
        packed = pack(spots[0], observed, 1, each, [0], crossed)
        packed, panels = lax.optimization_barrier((packed, panels))
    rows_panel, prior_panel, gram = panel_gram(rows, spots[0], panels, *priors)
    other_gram = handed_on(gram)
    if parts > 1:
        packed, first = lax.optimization_barrier((packed, first))
        second = over(packed)
        arrived.append((second, second))
    inverse = factor(gram, other_gram)
    rows_panel, inverse = lax.optimization_barrier((rows_panel, inverse))
    out = jnp.zeros((total // rows, rows, parts, each, LANES), jnp.float32)
    for part, (far, near) in enumerate(arrived):
        info = info_part(each, spots[part], rows_panel, prior_panel, prior, far, near)
        slab = slab_part(rows, spots[part], inverse, info, handed_on(info))
        slab = lax.all_to_all(slab, "row", 0, 0, tiled=True)
        slab = slab.reshape(rows, total // rows, each, LANES).transpose(1, 0, 2, 3)
        out = out.at[:, :, part].set(slab)
    out = out.reshape(total // rows, rows * chunk, LANES)[:, :blocks]
    return out.reshape(1, total // rows, cycles, 1, width)


def solution(mesh):
    placed = (
        P(None, None, "col", None),
        P("section", "row", None, "col", None),
        P("section", "row"),
    )
    return jax.shard_map(
        on_device,
        mesh=mesh,
        in_specs=placed,
        out_specs=P("section", "row", None, "col", None),
        check_vma=False,
    )
```

```python
import functools

import jax
import jax.numpy as jnp
from jax import lax
from jax.experimental import pallas as pl
from jax.experimental.pallas import tpu as pltpu
from jax.sharding import PartitionSpec as P

LANES = 128
TALL = 16
GROUP = 8
SPOTS = 6
VMEM_BYTES = 56 * 2**20


def dot(left, right, contract_left, contract_right):
    return lax.dot_general(
        left,
        right,
        (((contract_left,), (contract_right,)), ((), ())),
        precision=lax.Precision.HIGHEST,
        preferred_element_type=jnp.float32,
    )


def thirds(value):
    high = value.astype(jnp.bfloat16)
    rest = value - high.astype(jnp.float32)
    middle = rest.astype(jnp.bfloat16)
    return high, middle, (rest - middle.astype(jnp.float32)).astype(jnp.bfloat16)


def short_dot(left, right, contract_left, contract_right):
    a, b = thirds(left), thirds(right)
    left = jnp.concatenate([a[0], a[0], a[1], a[1], a[0], a[2]], axis=contract_left)
    right = jnp.concatenate([b[0], b[1], b[0], b[1], b[2], b[0]], axis=contract_right)
    return lax.dot_general(
        left,
        right,
        (((contract_left,), (contract_right,)), ((), ())),
        preferred_element_type=jnp.float32,
    )


def spread(row, shape):
    return jnp.broadcast_to(row, shape)


def factor_block(work_ref):
    size = work_ref.shape[0]
    tile = (8, LANES)
    row_ids = lax.broadcasted_iota(jnp.int32, tile, 0)
    for first in range(0, size, TALL):
        middle, end = first + 8, first + TALL
        top = [work_ref[first:middle, t * LANES : (t + 1) * LANES] for t in range(2)]
        low = [work_ref[middle:end, t * LANES : (t + 1) * LANES] for t in range(2)]
        top_col = [spread(top[0][:, first + k : first + k + 1], tile) for k in range(TALL)]
        low_col = [spread(low[0][:, first + k : first + k + 1], tile) for k in range(TALL)]
        top_pivot = jnp.ones(tile, jnp.float32)
        low_pivot = jnp.ones(tile, jnp.float32)
        for step in range(TALL):
            if step < 8:
                pivot = spread(top_col[step][step : step + 1], tile)
                inverse = 1.0 / pivot
                top_by = jnp.where(row_ids > step, top_col[step] * inverse, 0.0)
                low_by = low_col[step] * inverse
                top_pivot = jnp.where(row_ids == step, pivot, top_pivot)
                for k in range(step + 1, TALL):
                    lead = spread(top_col[k][step : step + 1], tile)
                    top_col[k] = top_col[k] - top_by * lead
                    low_col[k] = low_col[k] - low_by * lead
                for t in range(2):
                    lead = spread(top[t][step : step + 1], tile)
                    top[t] = top[t] - top_by * lead
                    low[t] = low[t] - low_by * lead
            else:
                at = step - 8
                pivot = spread(low_col[step][at : at + 1], tile)
                low_by = jnp.where(row_ids > at, low_col[step] * (1.0 / pivot), 0.0)
                low_pivot = jnp.where(row_ids == at, pivot, low_pivot)
                for k in range(step + 1, TALL):
                    low_col[k] = low_col[k] - low_by * spread(low_col[k][at : at + 1], tile)
                for t in range(2):
                    low[t] = low[t] - low_by * spread(low[t][at : at + 1], tile)
        top_scale, low_scale = lax.rsqrt(top_pivot), lax.rsqrt(low_pivot)
        for t in range(2):
            work_ref[first:middle, t * LANES : (t + 1) * LANES] = top[t] * top_scale
            work_ref[middle:end, t * LANES : (t + 1) * LANES] = low[t] * low_scale
        if end < size:
            done = work_ref[first:end, :]
            change = short_dot(done[:, :LANES], done, 0, 0)
            work_ref[end:, :] = work_ref[end:, :] - change[end:, :]


def factor_kernel(own_ref, other_ref, inverse_ref, info_ref, work_ref):
    size = own_ref.shape[0]
    ids = [lax.broadcasted_iota(jnp.int32, (LANES, LANES), axis) for axis in range(2)]
    eye = (ids[0] == ids[1]).astype(jnp.float32)
    info_ref[...] = own_ref[...] + other_ref[...]
    inverse_ref[...] = jnp.zeros_like(inverse_ref)
    for start in range(0, size, LANES):
        end = start + LANES
        work_ref[:, :LANES] = info_ref[start:end, start:end]
        work_ref[:, LANES:] = eye
        factor_block(work_ref)
        block = work_ref[:, LANES:]
        if start:
            inverse_ref[start:end, :start] = short_dot(block, inverse_ref[start:end, :start], 1, 0)
        inverse_ref[start:end, start:end] = block
        if end < size:
            upper = short_dot(block, info_ref[start:end, end:], 1, 0)
            info_ref[end:, end:] = info_ref[end:, end:] - short_dot(upper, upper, 0, 0)
            inverse_ref[end:, :end] = inverse_ref[end:, :end] - short_dot(
                upper, inverse_ref[start:end, :end], 0, 0
            )


def vmem_spec():
    return pl.BlockSpec(memory_space=pltpu.VMEM)


def params():
    return pltpu.CompilerParams(vmem_limit_bytes=VMEM_BYTES)


def shape_of(*shape):
    return jax.ShapeDtypeStruct(shape, jnp.float32)


def factor(own, other):
    size = own.shape[0]
    return pl.pallas_call(
        factor_kernel,
        out_shape=shape_of(size, size),
        in_specs=[vmem_spec()] * 2,
        out_specs=vmem_spec(),
        scratch_shapes=[
            pltpu.VMEM((size, size), jnp.float32),
            pltpu.VMEM((LANES, 2 * LANES), jnp.float32),
        ],
        compiler_params=params(),
        name="factor",
    )(own, other)


def prior_kernel(chunk, spot_ref, near_prior, far_prior, blocks_ref, info_ref, gram_ref, panel, work):
    total, group = blocks_ref.shape[0], blocks_ref.shape[1]
    width = near_prior.shape[1]
    col, section = spot_ref[0], spot_ref[1]
    near_at = pl.ds(pl.multiple_of(col * width, width), width)
    far_at = pl.ds(pl.multiple_of((1 - col) * width, width), width)
    keep = (section == 0).astype(jnp.float32)
    panel[:, near_at] = near_prior[...] * keep
    panel[:, far_at] = far_prior[...] * keep
    upper = panel[:width, :]
    gram_ref[:width, :] = dot(upper[:, :width], upper, 0, 0)
    corner = panel[:, width:]
    gram_ref[width:, width:] = dot(corner, corner, 0, 0)
    gram_ref[width:, :width] = jnp.zeros((width, width), jnp.float32)
    gather_blocks(blocks_ref.reshape(total * group, LANES), spot_ref[5], total, group, chunk, work, 0)
    info_ref[...] = dot(panel[...], work[...], 0, 0)


def prior_part(chunk, spot, near_prior, far_prior, prior):
    total, _, group, _ = prior.shape
    full = lambda array: pl.BlockSpec(array.shape, lambda i, spot: (0,) * array.ndim)
    out = (shape_of(total, chunk * LANES), shape_of(total, total))
    return pl.pallas_call(
        functools.partial(prior_kernel, chunk),
        out_shape=out,
        grid_spec=pltpu.PrefetchScalarGridSpec(
            num_scalar_prefetch=1,
            grid=(1,),
            in_specs=[
                full(near_prior),
                full(far_prior),
                pl.BlockSpec((total, None, group, LANES), lambda i, spot: (0, spot[4], 0, 0)),
            ],
            out_specs=[full(array) for array in out],
            scratch_shapes=[
                pltpu.VMEM((total, total), jnp.float32),
                pltpu.VMEM((total, chunk * LANES), jnp.float32),
            ],
        ),
        compiler_params=params(),
        name="prior_part",
    )(spot, near_prior, far_prior, prior)


def panel_kernel(count, spot_ref, near_ref, near_next, far_here, far_next, prior_ref, rows_ref, gram_ref):
    width = near_ref.shape[1]
    col = spot_ref[0]
    near_at = pl.ds(pl.multiple_of(col * width, width), width)
    far_at = pl.ds(pl.multiple_of((1 - col) * width, width), width)
    slots = near_ref.shape[0] * 2 // count
    pair = spot_ref[2] // 2
    for i in range(count // 2):
        here, beside = (pl.ds(((pair ^ i) + side) * slots, slots) for side in (0, count // 2))
        piece = slice(i * slots, (i + 1) * slots)
        rows_ref[here, near_at] = near_ref[piece]
        rows_ref[beside, near_at] = near_next[piece]
        rows_ref[here, far_at] = far_here[piece]
        rows_ref[beside, far_at] = far_next[piece]
    right = rows_ref[:, width:]
    gram_ref[:width, :] = prior_ref[:width, :] + dot(rows_ref[:, :width], rows_ref[...], 0, 0)
    gram_ref[width:, width:] = prior_ref[width:, width:] + dot(right, right, 0, 0)
    gram_ref[width:, :width] = jnp.zeros((width, width), jnp.float32)


def panel_gram(count, spot, parts, prior_gram):
    slots, total = parts[0].shape[0] * 2 // count, prior_gram.shape[0]
    return pl.pallas_call(
        functools.partial(panel_kernel, count),
        out_shape=(shape_of(count * slots, total), shape_of(total, total)),
        in_specs=[pl.BlockSpec(memory_space=pltpu.SMEM)] + [vmem_spec()] * 5,
        out_specs=(vmem_spec(),) * 2,
        compiler_params=params(),
        name="panel_gram",
    )(spot, *parts, prior_gram)


def gather_blocks(ref, first, rows, stride, blocks, work, at):
    for b in range(blocks):
        work[pl.ds(at, rows), b * LANES : (b + 1) * LANES] = ref[
            pl.ds(first + b, rows, stride=stride), :
        ]


def pack_kernel(first, each, joined, spot_ref, *refs):
    *sources, out_ref = refs
    outs = [out_ref] if len(out_ref.shape) == 2 else [out_ref.at[i] for i in range(2)]
    if joined:
        outs.pop(0)[...] = sources.pop(0)[...]
    for source, out in zip(sources, outs):
        slots, chunk, _ = source.shape
        flat = source.reshape(slots * chunk, LANES)
        for b in range(each):
            out[pl.ds(b, slots, stride=each), :] = flat[pl.ds(first + b, slots, stride=chunk), :]


def pack(spot, observed, part, each, sides, swapped_blocks=None):
    slots, rows, chunk, _ = observed.shape
    size = slots * each

    def source(side):
        at = lambda i, spot: (0, 2 * i + (spot[2] + side) % 2, 0, 0)
        return pl.BlockSpec((slots, None, chunk, LANES), at)

    specs, arrays = [source(side) for side in sides], [observed] * len(sides)
    if swapped_blocks is not None:
        specs = [pl.BlockSpec((None, size, LANES), lambda i, spot: (i, 0, 0))] + specs
        arrays = [swapped_blocks] + arrays
    if len(specs) == 1:
        out, out_spec = (rows // 2, size), pl.BlockSpec((None, size, LANES), lambda i, spot: (i, 0, 0))
    else:
        out = (rows // 2, 2, size)
        out_spec = pl.BlockSpec((None, 2, size, LANES), lambda i, spot: (i, 0, 0, 0))
    return pl.pallas_call(
        functools.partial(pack_kernel, part * each, each, swapped_blocks is not None),
        out_shape=shape_of(*out, LANES),
        grid_spec=pltpu.PrefetchScalarGridSpec(
            num_scalar_prefetch=1, grid=(rows // 2,), in_specs=specs, out_specs=out_spec
        ),
        compiler_params=params(),
        name="pack",
    )(spot, *arrays)


def plain_pack(spot, observed):
    slots, rows, chunk, _ = observed.shape
    pairs = observed.reshape(slots, rows // 2, 2, chunk, LANES).transpose(1, 2, 0, 3, 4)
    sides = [lax.dynamic_index_in_dim(pairs, (spot[2] + side) % 2, 1, keepdims=False) for side in (1, 0)]
    return jnp.stack(sides, axis=1).reshape(rows // 2, 2, slots * chunk, LANES)


def info_kernel(each, spot_ref, rows_ref, prior_ref, far_ref, near_ref, out_ref, work):
    count, pairs = rows_ref.shape[0], far_ref.shape[0]
    slots = count // 2 // pairs
    for i in range(pairs):
        gather_blocks(near_ref.at[i], 0, slots, each, each, work, i * slots)
        gather_blocks(far_ref.at[i], 0, slots, each, each, work, count // 2 + i * slots)
    out_ref[...] = prior_ref[...] + dot(rows_ref[...], work[...], 0, 0)


def info_part(part, each, spot, rows, prior_info, far, near):
    total = prior_info.shape[0]
    half = lambda array, at: pl.BlockSpec(
        (array.shape[0], None) + array.shape[2:], lambda i, spot: (0, at, 0, 0)
    )
    full = lambda array: pl.BlockSpec(array.shape, lambda i, spot: (0,) * array.ndim)
    return pl.pallas_call(
        functools.partial(info_kernel, each),
        out_shape=shape_of(total, each * LANES),
        grid_spec=pltpu.PrefetchScalarGridSpec(
            num_scalar_prefetch=1,
            grid=(1,),
            in_specs=[
                full(rows),
                pl.BlockSpec((total, each * LANES), lambda i, spot: (0, part)),
                full(far) if far.ndim == 3 else half(far, 0),
                half(near, 1),
            ],
            out_specs=pl.BlockSpec((total, each * LANES), lambda i, spot: (0, 0)),
            scratch_shapes=[pltpu.VMEM((rows.shape[0], each * LANES), jnp.float32)],
        ),
        compiler_params=params(),
        name="info_part",
    )(spot, rows, prior_info, far, near)


def slab_kernel(count, spot_ref, inverse_ref, own_ref, other_ref, out_ref):
    total, width = own_ref.shape
    own_rows, chunk = total // count, width // LANES
    half = total // 2
    tile = (own_rows, LANES)
    row_ids = lax.broadcasted_iota(jnp.int32, tile, 0)
    lane_ids = lax.broadcasted_iota(jnp.int32, tile, 1)
    info = own_ref[...] + other_ref[...]
    for side in range(2):
        depth = (side + 1) * half
        slab = dot(inverse_ref[side * half : depth, :depth], info[:depth, :], 1, 0)
        for b in range(chunk):
            for e in range(count // 2):
                d = side * (count // 2) + e
                part = slab[e * own_rows : (e + 1) * own_rows, b * LANES : (b + 1) * LANES]
                kept = jnp.where(spot_ref[SPOTS + b] + lane_ids >= row_ids + d * own_rows, part, 0.0)
                out_ref[d, pl.ds(b, own_rows, stride=chunk), :] = kept


def slab_part(count, spot, inverse, own, other):
    total, width = own.shape
    return pl.pallas_call(
        functools.partial(slab_kernel, count),
        out_shape=shape_of(count, total // count * width // LANES, LANES),
        in_specs=[pl.BlockSpec(memory_space=pltpu.SMEM)] + [vmem_spec()] * 3,
        out_specs=vmem_spec(),
        compiler_params=params(),
        name="slab_part",
    )(spot, inverse, own, other)


def swapped(value, axis, bits):
    count = lax.axis_size(axis)
    return lax.ppermute(value, axis, [(i, i ^ bits) for i in range(count)])


def handed_on(value):
    return lax.ppermute(value, "section", [(0, 1)])


def z_panels(near):
    rows = lax.axis_size("row")
    return jnp.concatenate([near] + [swapped(near, "row", k) for k in range(2, rows, 2)], axis=0)


def prior_panels(near_prior):
    if lax.axis_size("col") == 2:
        return near_prior, swapped(near_prior, "col", 1)
    priors = lax.all_gather(near_prior, "col")
    return priors[0], priors[1]


def all_panels(near):
    rows, cols = lax.axis_size("row"), lax.axis_size("col")
    if cols == 2:
        order = [(i, i ^ 3) for i in range(rows * cols)]
        far = [swapped(near, "col", 1), lax.ppermute(near, ("row", "col"), order)]
        return [near, swapped(near, "row", 1)] + far
    both = lax.all_gather(near, "col")
    both = [both[0], both[1]]
    beside = [swapped(panel, "row", 1) for panel in both]
    return [both[0], beside[0], both[1], beside[1]]


def on_device(prior_root, observations, live_rows):
    total, cycles, _, width = prior_root.shape
    slots = observations.shape[1]
    rows, cols = lax.axis_size("row"), lax.axis_size("col")
    per = width // LANES
    blocks = cycles * per
    chunk = -(-blocks // rows)
    parts = 2 if chunk % GROUP == 0 else 1
    each = chunk // parts
    col, row, section = (lax.axis_index(axis) for axis in ("col", "row", "section"))
    group = min(GROUP, chunk * rows)

    def spot_of(part):
        first = row * chunk + part * each
        spot = [col if cols == 2 else 0, section, row, 0, first // group, first % group]
        spot += [((first + b) // per * cols + col) * width + (first + b) % per * LANES for b in range(each)]
        return jnp.stack([jnp.asarray(value, jnp.int32) for value in spot])

    def in_blocks(array):
        array = array.reshape(array.shape[0], blocks, LANES)
        return jnp.pad(array, ((0, 0), (0, chunk * rows - blocks), (0, 0)))

    spots = [spot_of(part) for part in range(parts)]
    prior = in_blocks(prior_root.reshape(total, -1)).reshape(total, -1, group, LANES)
    observed = in_blocks(observations.reshape(slots, -1)).reshape(slots, rows, chunk, LANES)
    live = lax.broadcasted_iota(jnp.int32, (slots, 1), 0) < live_rows[0, 0]
    near = jnp.where(live, observations[0, :, 0, 0, :], 0.0)
    same_side = [[2 * i + side for i in range(rows // 2)] for side in range(2)]

    def over(piece):
        return lax.all_to_all(piece, "row", 0, 0, axis_index_groups=same_side, tiled=True)

    near = z_panels(near)
    priors = prior_panels(prior_root[:, 0, 0, :])
    if parts > 1:
        crossing = pack(spots[0], observed, 1, each, [1])
        packed = pack(spots[0], observed, 0, each, [1, 0])
        packed, crossing, near = lax.optimization_barrier((packed, crossing, near))
        crossed = swapped(crossing, "row", 1)
        near, priors = lax.optimization_barrier((near, priors))
    else:
        packed, near = lax.optimization_barrier((plain_pack(spots[0], observed), near))
    panels = all_panels(near)
    first = over(packed)
    far = first[:, 0]
    far, _ = lax.optimization_barrier((far, panels))
    arrived = [(swapped(far, "row", 1), first)]
    prior_info, prior_gram = prior_part(chunk, spots[0], *priors, prior)
    if parts > 1:
        observed, prior_gram = lax.optimization_barrier((observed, prior_gram))
        packed = pack(spots[0], observed, 1, each, [0], crossed)
        packed, panels = lax.optimization_barrier((packed, panels))
    rows_panel, gram = panel_gram(rows, spots[0], panels, prior_gram)
    other_gram = handed_on(gram)
    if parts > 1:
        packed, first = lax.optimization_barrier((packed, first))
        second = over(packed)
        arrived.append((second, second))
    inverse = factor(gram, other_gram)
    rows_panel, inverse = lax.optimization_barrier((rows_panel, inverse))
    out = jnp.zeros((total // rows, rows, parts, each, LANES), jnp.float32)
    for part, (far, near) in enumerate(arrived):
        if part:
            rows_panel, other = lax.optimization_barrier((rows_panel, other))
        info = info_part(part, each, spots[part], rows_panel, prior_info, far, near)
        other = handed_on(info)
        slab = slab_part(rows, spots[part], inverse, info, other)
        slab = lax.all_to_all(slab, "row", 0, 0, tiled=True)
        slab = slab.reshape(rows, total // rows, each, LANES).transpose(1, 0, 2, 3)
        out = out.at[:, :, part].set(slab)
    out = out.reshape(total // rows, rows * chunk, LANES)[:, :blocks]
    return out.reshape(1, total // rows, cycles, 1, width)


def solution(mesh):
    placed = (
        P(None, None, "col", None),
        P("section", "row", None, "col", None),
        P("section", "row"),
    )
    return jax.shard_map(
        on_device,
        mesh=mesh,
        in_specs=placed,
        out_specs=P("section", "row", None, "col", None),
        check_vma=False,
    )
```

```python
import functools

import jax
import jax.numpy as jnp
from jax import lax
from jax.experimental import pallas as pl
from jax.experimental.pallas import tpu as pltpu
from jax.sharding import PartitionSpec as P

LANES = 128
TALL = 16
GROUP = 8
SPOTS = 6
VMEM_BYTES = 56 * 2**20


def dot(left, right, contract_left, contract_right):
    return lax.dot_general(
        left,
        right,
        (((contract_left,), (contract_right,)), ((), ())),
        precision=lax.Precision.HIGHEST,
        preferred_element_type=jnp.float32,
    )


def thirds(value):
    high = value.astype(jnp.bfloat16)
    rest = value - high.astype(jnp.float32)
    middle = rest.astype(jnp.bfloat16)
    return high, middle, (rest - middle.astype(jnp.float32)).astype(jnp.bfloat16)


def short_dot(left, right, contract_left, contract_right):
    a, b = thirds(left), thirds(right)
    left = jnp.concatenate([a[0], a[0], a[1], a[1], a[0], a[2]], axis=contract_left)
    right = jnp.concatenate([b[0], b[1], b[0], b[1], b[2], b[0]], axis=contract_right)
    return lax.dot_general(
        left,
        right,
        (((contract_left,), (contract_right,)), ((), ())),
        preferred_element_type=jnp.float32,
    )


def spread(row, shape):
    return jnp.broadcast_to(row, shape)


def factor_block(work_ref):
    size = work_ref.shape[0]
    tile = (8, LANES)
    row_ids = lax.broadcasted_iota(jnp.int32, tile, 0)
    for first in range(0, size, TALL):
        middle, end = first + 8, first + TALL
        top = [work_ref[first:middle, t * LANES : (t + 1) * LANES] for t in range(2)]
        low = [work_ref[middle:end, t * LANES : (t + 1) * LANES] for t in range(2)]
        top_col = [spread(top[0][:, first + k : first + k + 1], tile) for k in range(TALL)]
        low_col = [spread(low[0][:, first + k : first + k + 1], tile) for k in range(TALL)]
        top_pivot = jnp.ones(tile, jnp.float32)
        low_pivot = jnp.ones(tile, jnp.float32)
        for step in range(TALL):
            if step < 8:
                pivot = spread(top_col[step][step : step + 1], tile)
                inverse = 1.0 / pivot
                top_by = jnp.where(row_ids > step, top_col[step] * inverse, 0.0)
                low_by = low_col[step] * inverse
                top_pivot = jnp.where(row_ids == step, pivot, top_pivot)
                for k in range(step + 1, TALL):
                    lead = spread(top_col[k][step : step + 1], tile)
                    top_col[k] = top_col[k] - top_by * lead
                    low_col[k] = low_col[k] - low_by * lead
                for t in range(2):
                    lead = spread(top[t][step : step + 1], tile)
                    top[t] = top[t] - top_by * lead
                    low[t] = low[t] - low_by * lead
            else:
                at = step - 8
                pivot = spread(low_col[step][at : at + 1], tile)
                low_by = jnp.where(row_ids > at, low_col[step] * (1.0 / pivot), 0.0)
                low_pivot = jnp.where(row_ids == at, pivot, low_pivot)
                for k in range(step + 1, TALL):
                    low_col[k] = low_col[k] - low_by * spread(low_col[k][at : at + 1], tile)
                for t in range(2):
                    low[t] = low[t] - low_by * spread(low[t][at : at + 1], tile)
        top_scale, low_scale = lax.rsqrt(top_pivot), lax.rsqrt(low_pivot)
        for t in range(2):
            work_ref[first:middle, t * LANES : (t + 1) * LANES] = top[t] * top_scale
            work_ref[middle:end, t * LANES : (t + 1) * LANES] = low[t] * low_scale
        if end < size:
            done = work_ref[first:end, :]
            change = short_dot(done[:, :LANES], done, 0, 0)
            work_ref[end:, :] = work_ref[end:, :] - change[end:, :]


def factor_kernel(own_ref, other_ref, inverse_ref, info_ref, work_ref):
    size = own_ref.shape[0]
    ids = [lax.broadcasted_iota(jnp.int32, (LANES, LANES), axis) for axis in range(2)]
    eye = (ids[0] == ids[1]).astype(jnp.float32)
    info_ref[...] = own_ref[...] + other_ref[...]
    inverse_ref[...] = jnp.zeros_like(inverse_ref)
    for start in range(0, size, LANES):
        end = start + LANES
        work_ref[:, :LANES] = info_ref[start:end, start:end]
        work_ref[:, LANES:] = eye
        factor_block(work_ref)
        block = work_ref[:, LANES:]
        if start:
            inverse_ref[start:end, :start] = short_dot(block, inverse_ref[start:end, :start], 1, 0)
        inverse_ref[start:end, start:end] = block
        if end < size:
            upper = short_dot(block, info_ref[start:end, end:], 1, 0)
            info_ref[end:, end:] = info_ref[end:, end:] - short_dot(upper, upper, 0, 0)
            inverse_ref[end:, :end] = inverse_ref[end:, :end] - short_dot(
                upper, inverse_ref[start:end, :end], 0, 0
            )


def vmem_spec():
    return pl.BlockSpec(memory_space=pltpu.VMEM)


def params():
    return pltpu.CompilerParams(vmem_limit_bytes=VMEM_BYTES)


def shape_of(*shape):
    return jax.ShapeDtypeStruct(shape, jnp.float32)


def factor(own, other):
    size = own.shape[0]
    return pl.pallas_call(
        factor_kernel,
        out_shape=shape_of(size, size),
        in_specs=[vmem_spec()] * 2,
        out_specs=vmem_spec(),
        scratch_shapes=[
            pltpu.VMEM((size, size), jnp.float32),
            pltpu.VMEM((LANES, 2 * LANES), jnp.float32),
        ],
        compiler_params=params(),
        name="factor",
    )(own, other)


def prior_kernel(chunk, spot_ref, near_prior, far_prior, blocks_ref, info_ref, gram_ref, panel, work):
    total, group = blocks_ref.shape[0], blocks_ref.shape[1]
    width = near_prior.shape[1]
    col, section = spot_ref[0], spot_ref[1]
    near_at = pl.ds(pl.multiple_of(col * width, width), width)
    far_at = pl.ds(pl.multiple_of((1 - col) * width, width), width)
    keep = (section == 0).astype(jnp.float32)
    panel[:, near_at] = near_prior[...] * keep
    panel[:, far_at] = far_prior[...] * keep
    upper = panel[:width, :]
    gram_ref[:width, :] = dot(upper[:, :width], upper, 0, 0)
    corner = panel[:, width:]
    gram_ref[width:, width:] = dot(corner, corner, 0, 0)
    gram_ref[width:, :width] = jnp.zeros((width, width), jnp.float32)
    gather_blocks(blocks_ref.reshape(total * group, LANES), spot_ref[5], total, group, chunk, work, 0)
    info_ref[...] = dot(panel[...], work[...], 0, 0)


def prior_part(chunk, spot, near_prior, far_prior, prior):
    total, _, group, _ = prior.shape
    full = lambda array: pl.BlockSpec(array.shape, lambda i, spot: (0,) * array.ndim)
    out = (shape_of(total, chunk * LANES), shape_of(total, total))
    return pl.pallas_call(
        functools.partial(prior_kernel, chunk),
        out_shape=out,
        grid_spec=pltpu.PrefetchScalarGridSpec(
            num_scalar_prefetch=1,
            grid=(1,),
            in_specs=[
                full(near_prior),
                full(far_prior),
                pl.BlockSpec((total, None, group, LANES), lambda i, spot: (0, spot[4], 0, 0)),
            ],
            out_specs=[full(array) for array in out],
            scratch_shapes=[
                pltpu.VMEM((total, total), jnp.float32),
                pltpu.VMEM((total, chunk * LANES), jnp.float32),
            ],
        ),
        compiler_params=params(),
        name="prior_part",
    )(spot, near_prior, far_prior, prior)


def panel_kernel(count, spot_ref, near_ref, near_next, far_here, far_next, prior_ref, rows_ref, gram_ref):
    width = near_ref.shape[1]
    col = spot_ref[0]
    near_at = pl.ds(pl.multiple_of(col * width, width), width)
    far_at = pl.ds(pl.multiple_of((1 - col) * width, width), width)
    slots = near_ref.shape[0] * 2 // count
    pair = spot_ref[2] // 2
    for i in range(count // 2):
        here, beside = (pl.ds(((pair ^ i) + side) * slots, slots) for side in (0, count // 2))
        piece = slice(i * slots, (i + 1) * slots)
        rows_ref[here, near_at] = near_ref[piece]
        rows_ref[beside, near_at] = near_next[piece]
        rows_ref[here, far_at] = far_here[piece]
        rows_ref[beside, far_at] = far_next[piece]
    right = rows_ref[:, width:]
    gram_ref[:width, :] = prior_ref[:width, :] + dot(rows_ref[:, :width], rows_ref[...], 0, 0)
    gram_ref[width:, width:] = prior_ref[width:, width:] + dot(right, right, 0, 0)
    gram_ref[width:, :width] = jnp.zeros((width, width), jnp.float32)


def panel_gram(count, spot, parts, prior_gram):
    slots, total = parts[0].shape[0] * 2 // count, prior_gram.shape[0]
    return pl.pallas_call(
        functools.partial(panel_kernel, count),
        out_shape=(shape_of(count * slots, total), shape_of(total, total)),
        in_specs=[pl.BlockSpec(memory_space=pltpu.SMEM)] + [vmem_spec()] * 5,
        out_specs=(vmem_spec(),) * 2,
        compiler_params=params(),
        name="panel_gram",
    )(spot, *parts, prior_gram)


def gather_blocks(ref, first, rows, stride, blocks, work, at):
    for b in range(blocks):
        work[pl.ds(at, rows), b * LANES : (b + 1) * LANES] = ref[
            pl.ds(first + b, rows, stride=stride), :
        ]


def pack_kernel(first, each, joined, spot_ref, *refs):
    *sources, out_ref = refs
    outs = [out_ref] if len(out_ref.shape) == 2 else [out_ref.at[i] for i in range(2)]
    if joined:
        outs.pop(0)[...] = sources.pop(0)[...]
    for source, out in zip(sources, outs):
        slots, chunk, _ = source.shape
        flat = source.reshape(slots * chunk, LANES)
        for b in range(each):
            out[pl.ds(b, slots, stride=each), :] = flat[pl.ds(first + b, slots, stride=chunk), :]


def pack(spot, observed, part, each, sides, swapped_blocks=None):
    slots, rows, chunk, _ = observed.shape
    size = slots * each

    def source(side):
        at = lambda i, spot: (0, 2 * i + (spot[2] + side) % 2, 0, 0)
        return pl.BlockSpec((slots, None, chunk, LANES), at)

    specs, arrays = [source(side) for side in sides], [observed] * len(sides)
    if swapped_blocks is not None:
        specs = [pl.BlockSpec((None, size, LANES), lambda i, spot: (i, 0, 0))] + specs
        arrays = [swapped_blocks] + arrays
    if len(specs) == 1:
        out, out_spec = (rows // 2, size), pl.BlockSpec((None, size, LANES), lambda i, spot: (i, 0, 0))
    else:
        out = (rows // 2, 2, size)
        out_spec = pl.BlockSpec((None, 2, size, LANES), lambda i, spot: (i, 0, 0, 0))
    return pl.pallas_call(
        functools.partial(pack_kernel, part * each, each, swapped_blocks is not None),
        out_shape=shape_of(*out, LANES),
        grid_spec=pltpu.PrefetchScalarGridSpec(
            num_scalar_prefetch=1, grid=(rows // 2,), in_specs=specs, out_specs=out_spec
        ),
        compiler_params=params(),
        name="pack",
    )(spot, *arrays)


def plain_pack(spot, observed):
    slots, rows, chunk, _ = observed.shape
    pairs = observed.reshape(slots, rows // 2, 2, chunk, LANES).transpose(1, 2, 0, 3, 4)
    sides = [lax.dynamic_index_in_dim(pairs, (spot[2] + side) % 2, 1, keepdims=False) for side in (1, 0)]
    return jnp.stack(sides, axis=1).reshape(rows // 2, 2, slots * chunk, LANES)


def info_kernel(each, spot_ref, rows_ref, prior_ref, far_ref, near_ref, out_ref, work):
    count, pairs = rows_ref.shape[0], far_ref.shape[0]
    slots = count // 2 // pairs
    for i in range(pairs):
        gather_blocks(near_ref.at[i], 0, slots, each, each, work, i * slots)
        gather_blocks(far_ref.at[i], 0, slots, each, each, work, count // 2 + i * slots)
    out_ref[...] = prior_ref[...] + dot(rows_ref[...], work[...], 0, 0)


def info_part(part, each, spot, rows, prior_info, far, near):
    total = prior_info.shape[0]
    half = lambda array, at: pl.BlockSpec(
        (array.shape[0], None) + array.shape[2:], lambda i, spot: (0, at, 0, 0)
    )
    full = lambda array: pl.BlockSpec(array.shape, lambda i, spot: (0,) * array.ndim)
    return pl.pallas_call(
        functools.partial(info_kernel, each),
        out_shape=shape_of(total, each * LANES),
        grid_spec=pltpu.PrefetchScalarGridSpec(
            num_scalar_prefetch=1,
            grid=(1,),
            in_specs=[
                full(rows),
                pl.BlockSpec((total, each * LANES), lambda i, spot: (0, part)),
                full(far) if far.ndim == 3 else half(far, 0),
                half(near, 1),
            ],
            out_specs=pl.BlockSpec((total, each * LANES), lambda i, spot: (0, 0)),
            scratch_shapes=[pltpu.VMEM((rows.shape[0], each * LANES), jnp.float32)],
        ),
        compiler_params=params(),
        name="info_part",
    )(spot, rows, prior_info, far, near)


def slab_kernel(count, spot_ref, inverse_ref, own_ref, other_ref, out_ref):
    total, width = own_ref.shape
    own_rows, chunk = total // count, width // LANES
    half = total // 2
    tile = (own_rows, LANES)
    row_ids = lax.broadcasted_iota(jnp.int32, tile, 0)
    lane_ids = lax.broadcasted_iota(jnp.int32, tile, 1)
    info = own_ref[...] + other_ref[...]
    for side in range(2):
        depth = (side + 1) * half
        slab = dot(inverse_ref[side * half : depth, :depth], info[:depth, :], 1, 0)
        for b in range(chunk):
            for e in range(count // 2):
                d = side * (count // 2) + e
                part = slab[e * own_rows : (e + 1) * own_rows, b * LANES : (b + 1) * LANES]
                kept = jnp.where(spot_ref[SPOTS + b] + lane_ids >= row_ids + d * own_rows, part, 0.0)
                out_ref[d, pl.ds(b, own_rows, stride=chunk), :] = kept


def slab_part(count, spot, inverse, own, other):
    total, width = own.shape
    return pl.pallas_call(
        functools.partial(slab_kernel, count),
        out_shape=shape_of(count, total // count * width // LANES, LANES),
        in_specs=[pl.BlockSpec(memory_space=pltpu.SMEM)] + [vmem_spec()] * 3,
        out_specs=vmem_spec(),
        compiler_params=params(),
        name="slab_part",
    )(spot, inverse, own, other)


def sides_kernel(count, spot_ref, inverse_ref, own_ref, other_ref, near_ref, far_ref, work):
    total, width = own_ref.shape
    own_rows, chunk = total // count, width // LANES
    half = total // 2
    tile = (own_rows, LANES)
    row_ids = lax.broadcasted_iota(jnp.int32, tile, 0)
    lane_ids = lax.broadcasted_iota(jnp.int32, tile, 1)
    info = own_ref[...] + other_ref[...]
    for lower in range(2):
        depth = (lower + 1) * half
        work[lower * half : depth, :] = dot(inverse_ref[lower * half : depth, :depth], info[:depth, :], 1, 0)
    for change, out_ref in enumerate((near_ref, far_ref)):
        for pair in range(count // 2):
            first = pl.multiple_of((2 * pair + (spot_ref[2] + change) % 2) * own_rows, own_rows)
            for b in range(chunk):
                part = work[pl.ds(first, own_rows), b * LANES : (b + 1) * LANES]
                kept = jnp.where(spot_ref[SPOTS + b] + lane_ids >= row_ids + first, part, 0.0)
                out_ref[pair, pl.ds(b, own_rows, stride=chunk), :] = kept


def slab_sides(count, spot, inverse, own, other):
    total, width = own.shape
    out = shape_of(count // 2, total // count * width // LANES, LANES)
    return pl.pallas_call(
        functools.partial(sides_kernel, count),
        out_shape=(out, out),
        in_specs=[pl.BlockSpec(memory_space=pltpu.SMEM)] + [vmem_spec()] * 3,
        out_specs=(vmem_spec(),) * 2,
        scratch_shapes=[pltpu.VMEM((total, width), jnp.float32)],
        compiler_params=params(),
        name="slab_sides",
    )(spot, inverse, own, other)


def swapped(value, axis, bits):
    count = lax.axis_size(axis)
    return lax.ppermute(value, axis, [(i, i ^ bits) for i in range(count)])


def handed_on(value):
    return lax.ppermute(value, "section", [(0, 1)])


def z_panels(near):
    rows = lax.axis_size("row")
    return jnp.concatenate([near] + [swapped(near, "row", k) for k in range(2, rows, 2)], axis=0)


def prior_panels(near_prior):
    if lax.axis_size("col") == 2:
        return near_prior, swapped(near_prior, "col", 1)
    priors = lax.all_gather(near_prior, "col")
    return priors[0], priors[1]


def all_panels(near):
    rows, cols = lax.axis_size("row"), lax.axis_size("col")
    if cols == 2:
        order = [(i, i ^ 3) for i in range(rows * cols)]
        far = [swapped(near, "col", 1), lax.ppermute(near, ("row", "col"), order)]
        return [near, swapped(near, "row", 1)] + far
    both = lax.all_gather(near, "col")
    both = [both[0], both[1]]
    beside = [swapped(panel, "row", 1) for panel in both]
    return [both[0], beside[0], both[1], beside[1]]


def on_device(prior_root, observations, live_rows):
    total, cycles, _, width = prior_root.shape
    slots = observations.shape[1]
    rows, cols = lax.axis_size("row"), lax.axis_size("col")
    per = width // LANES
    blocks = cycles * per
    chunk = -(-blocks // rows)
    parts = 2 if chunk % GROUP == 0 else 1
    each = chunk // parts
    col, row, section = (lax.axis_index(axis) for axis in ("col", "row", "section"))
    group = min(GROUP, chunk * rows)

    def spot_of(part):
        first = row * chunk + part * each
        spot = [col if cols == 2 else 0, section, row, 0, first // group, first % group]
        spot += [((first + b) // per * cols + col) * width + (first + b) % per * LANES for b in range(each)]
        return jnp.stack([jnp.asarray(value, jnp.int32) for value in spot])

    def in_blocks(array):
        array = array.reshape(array.shape[0], blocks, LANES)
        return jnp.pad(array, ((0, 0), (0, chunk * rows - blocks), (0, 0)))

    spots = [spot_of(part) for part in range(parts)]
    prior = in_blocks(prior_root.reshape(total, -1)).reshape(total, -1, group, LANES)
    observed = in_blocks(observations.reshape(slots, -1)).reshape(slots, rows, chunk, LANES)
    live = lax.broadcasted_iota(jnp.int32, (slots, 1), 0) < live_rows[0, 0]
    near = jnp.where(live, observations[0, :, 0, 0, :], 0.0)
    same_side = [[2 * i + side for i in range(rows // 2)] for side in range(2)]

    def over(piece):
        return lax.all_to_all(piece, "row", 0, 0, axis_index_groups=same_side, tiled=True)

    near = z_panels(near)
    priors = prior_panels(prior_root[:, 0, 0, :])
    if parts > 1:
        crossing = pack(spots[0], observed, 1, each, [1])
        packed = pack(spots[0], observed, 0, each, [1, 0])
        packed, crossing, near = lax.optimization_barrier((packed, crossing, near))
        crossed = swapped(crossing, "row", 1)
        near, priors = lax.optimization_barrier((near, priors))
    else:
        packed, near = lax.optimization_barrier((plain_pack(spots[0], observed), near))
    panels = all_panels(near)
    first = over(packed)
    far = first[:, 0]
    far, _ = lax.optimization_barrier((far, panels))
    arrived = [(swapped(far, "row", 1), first)]
    prior_info, prior_gram = prior_part(chunk, spots[0], *priors, prior)
    if parts > 1:
        observed, prior_gram = lax.optimization_barrier((observed, prior_gram))
        packed = pack(spots[0], observed, 1, each, [0], crossed)
        packed, panels = lax.optimization_barrier((packed, panels))
    rows_panel, gram = panel_gram(rows, spots[0], panels, prior_gram)
    other_gram = handed_on(gram)
    if parts > 1:
        packed, first = lax.optimization_barrier((packed, first))
        second = over(packed)
        arrived.append((second, second))
    inverse = factor(gram, other_gram)
    rows_panel, inverse = lax.optimization_barrier((rows_panel, inverse))
    out = jnp.zeros((total // rows, rows, parts, each, LANES), jnp.float32)
    for part, (far, near) in enumerate(arrived):
        if part:
            rows_panel, other = lax.optimization_barrier((rows_panel, other))
        info = info_part(part, each, spots[part], rows_panel, prior_info, far, near)
        other = handed_on(info)
        if part == 0:
            slab = slab_part(rows, spots[part], inverse, info, other)
            slab = lax.all_to_all(slab, "row", 0, 0, tiled=True)
            continue
        sides = list(slab_sides(rows, spots[part], inverse, info, other))
        sides[1] = swapped(sides[1], "row", 1)
        placed = []
        for change, side in enumerate(sides):
            for k in range(rows // 2):
                piece = lax.dynamic_index_in_dim(side, (row // 2) ^ k, 0, keepdims=False)
                piece = swapped(piece, "row", 2 * k) if k else piece
                placed.append((row ^ (2 * k + change), piece.reshape(total // rows, each, LANES)))
        slab, received = lax.optimization_barrier((slab, [piece for _, piece in placed]))
        placed = [(source, piece) for (source, _), piece in zip(placed, received)]
    slab = slab.reshape(rows, total // rows, each, LANES).transpose(1, 0, 2, 3)
    out = out.at[:, :, 0].set(slab)
    if parts > 1:
        out = out.reshape(total // rows, rows * parts, each, LANES)
        for source, piece in placed:
            out = lax.dynamic_update_index_in_dim(out, piece, source * parts + 1, 1)
    out = out.reshape(total // rows, rows * chunk, LANES)[:, :blocks]
    return out.reshape(1, total // rows, cycles, 1, width)


def solution(mesh):
    placed = (
        P(None, None, "col", None),
        P("section", "row", None, "col", None),
        P("section", "row"),
    )
    return jax.shard_map(
        on_device,
        mesh=mesh,
        in_specs=placed,
        out_specs=P("section", "row", None, "col", None),
        check_vma=False,
    )
```

```python
import functools

import jax
import jax.numpy as jnp
from jax import lax
from jax.experimental import pallas as pl
from jax.experimental.pallas import tpu as pltpu
from jax.sharding import PartitionSpec as P

LANES = 128
TALL = 16
GROUP = 8
SPOTS = 6
VMEM_BYTES = 56 * 2**20


def dot(left, right, contract_left, contract_right):
    return lax.dot_general(
        left,
        right,
        (((contract_left,), (contract_right,)), ((), ())),
        precision=lax.Precision.HIGHEST,
        preferred_element_type=jnp.float32,
    )


def thirds(value):
    high = value.astype(jnp.bfloat16)
    rest = value - high.astype(jnp.float32)
    middle = rest.astype(jnp.bfloat16)
    return high, middle, (rest - middle.astype(jnp.float32)).astype(jnp.bfloat16)


def short_dot(left, right, contract_left, contract_right):
    a, b = thirds(left), thirds(right)
    left = jnp.concatenate([a[0], a[0], a[1], a[1], a[0], a[2]], axis=contract_left)
    right = jnp.concatenate([b[0], b[1], b[0], b[1], b[2], b[0]], axis=contract_right)
    return lax.dot_general(
        left,
        right,
        (((contract_left,), (contract_right,)), ((), ())),
        preferred_element_type=jnp.float32,
    )


def spread(row, shape):
    return jnp.broadcast_to(row, shape)


def factor_block(work_ref):
    size = work_ref.shape[0]
    tile = (8, LANES)
    row_ids = lax.broadcasted_iota(jnp.int32, tile, 0)
    for first in range(0, size, TALL):
        middle, end = first + 8, first + TALL
        top = [work_ref[first:middle, t * LANES : (t + 1) * LANES] for t in range(2)]
        low = [work_ref[middle:end, t * LANES : (t + 1) * LANES] for t in range(2)]
        top_col = [spread(top[0][:, first + k : first + k + 1], tile) for k in range(TALL)]
        low_col = [spread(low[0][:, first + k : first + k + 1], tile) for k in range(TALL)]
        top_pivot = jnp.ones(tile, jnp.float32)
        low_pivot = jnp.ones(tile, jnp.float32)
        for step in range(TALL):
            if step < 8:
                pivot = spread(top_col[step][step : step + 1], tile)
                inverse = 1.0 / pivot
                top_by = jnp.where(row_ids > step, top_col[step] * inverse, 0.0)
                low_by = low_col[step] * inverse
                top_pivot = jnp.where(row_ids == step, pivot, top_pivot)
                for k in range(step + 1, TALL):
                    lead = spread(top_col[k][step : step + 1], tile)
                    top_col[k] = top_col[k] - top_by * lead
                    low_col[k] = low_col[k] - low_by * lead
                for t in range(2):
                    lead = spread(top[t][step : step + 1], tile)
                    top[t] = top[t] - top_by * lead
                    low[t] = low[t] - low_by * lead
            else:
                at = step - 8
                pivot = spread(low_col[step][at : at + 1], tile)
                low_by = jnp.where(row_ids > at, low_col[step] * (1.0 / pivot), 0.0)
                low_pivot = jnp.where(row_ids == at, pivot, low_pivot)
                for k in range(step + 1, TALL):
                    low_col[k] = low_col[k] - low_by * spread(low_col[k][at : at + 1], tile)
                for t in range(2):
                    low[t] = low[t] - low_by * spread(low[t][at : at + 1], tile)
        top_scale, low_scale = lax.rsqrt(top_pivot), lax.rsqrt(low_pivot)
        for t in range(2):
            work_ref[first:middle, t * LANES : (t + 1) * LANES] = top[t] * top_scale
            work_ref[middle:end, t * LANES : (t + 1) * LANES] = low[t] * low_scale
        if end < size:
            done = work_ref[first:end, :]
            change = short_dot(done[:, :LANES], done, 0, 0)
            work_ref[end:, :] = work_ref[end:, :] - change[end:, :]


def factor_kernel(own_ref, other_ref, inverse_ref, info_ref, work_ref):
    size = own_ref.shape[0]
    ids = [lax.broadcasted_iota(jnp.int32, (LANES, LANES), axis) for axis in range(2)]
    eye = (ids[0] == ids[1]).astype(jnp.float32)
    info_ref[...] = own_ref[...] + other_ref[...]
    inverse_ref[...] = jnp.zeros_like(inverse_ref)
    for start in range(0, size, LANES):
        end = start + LANES
        work_ref[:, :LANES] = info_ref[start:end, start:end]
        work_ref[:, LANES:] = eye
        factor_block(work_ref)
        block = work_ref[:, LANES:]
        if start:
            inverse_ref[start:end, :start] = short_dot(block, inverse_ref[start:end, :start], 1, 0)
        inverse_ref[start:end, start:end] = block
        if end < size:
            upper = short_dot(block, info_ref[start:end, end:], 1, 0)
            info_ref[end:, end:] = info_ref[end:, end:] - short_dot(upper, upper, 0, 0)
            inverse_ref[end:, :end] = inverse_ref[end:, :end] - short_dot(
                upper, inverse_ref[start:end, :end], 0, 0
            )


def vmem_spec():
    return pl.BlockSpec(memory_space=pltpu.VMEM)


def params():
    return pltpu.CompilerParams(vmem_limit_bytes=VMEM_BYTES)


def shape_of(*shape):
    return jax.ShapeDtypeStruct(shape, jnp.float32)


def factor(own, other):
    size = own.shape[0]
    return pl.pallas_call(
        factor_kernel,
        out_shape=shape_of(size, size),
        in_specs=[vmem_spec()] * 2,
        out_specs=vmem_spec(),
        scratch_shapes=[
            pltpu.VMEM((size, size), jnp.float32),
            pltpu.VMEM((LANES, 2 * LANES), jnp.float32),
        ],
        compiler_params=params(),
        name="factor",
    )(own, other)


def prior_kernel(chunk, spot_ref, near_prior, far_prior, blocks_ref, info_ref, gram_ref, panel, work):
    total, group = blocks_ref.shape[0], blocks_ref.shape[1]
    width = near_prior.shape[1]
    col, section = spot_ref[0], spot_ref[1]
    near_at = pl.ds(pl.multiple_of(col * width, width), width)
    far_at = pl.ds(pl.multiple_of((1 - col) * width, width), width)
    keep = (section == 0).astype(jnp.float32)
    panel[:, near_at] = near_prior[...] * keep
    panel[:, far_at] = far_prior[...] * keep
    upper = panel[:width, :]
    gram_ref[:width, :] = dot(upper[:, :width], upper, 0, 0)
    corner = panel[:, width:]
    gram_ref[width:, width:] = dot(corner, corner, 0, 0)
    gram_ref[width:, :width] = jnp.zeros((width, width), jnp.float32)
    gather_blocks(blocks_ref.reshape(total * group, LANES), spot_ref[5], total, group, chunk, work, 0)
    info_ref[...] = dot(panel[...], work[...], 0, 0)


def prior_part(chunk, spot, near_prior, far_prior, prior):
    total, _, group, _ = prior.shape
    full = lambda array: pl.BlockSpec(array.shape, lambda i, spot: (0,) * array.ndim)
    out = (shape_of(total, chunk * LANES), shape_of(total, total))
    return pl.pallas_call(
        functools.partial(prior_kernel, chunk),
        out_shape=out,
        grid_spec=pltpu.PrefetchScalarGridSpec(
            num_scalar_prefetch=1,
            grid=(1,),
            in_specs=[
                full(near_prior),
                full(far_prior),
                pl.BlockSpec((total, None, group, LANES), lambda i, spot: (0, spot[4], 0, 0)),
            ],
            out_specs=[full(array) for array in out],
            scratch_shapes=[
                pltpu.VMEM((total, total), jnp.float32),
                pltpu.VMEM((total, chunk * LANES), jnp.float32),
            ],
        ),
        compiler_params=params(),
        name="prior_part",
    )(spot, near_prior, far_prior, prior)


def panel_kernel(count, spot_ref, near_ref, near_next, far_here, far_next, prior_ref, rows_ref, gram_ref):
    width = near_ref.shape[1]
    col = spot_ref[0]
    near_at = pl.ds(pl.multiple_of(col * width, width), width)
    far_at = pl.ds(pl.multiple_of((1 - col) * width, width), width)
    slots = near_ref.shape[0] * 2 // count
    pair = spot_ref[2] // 2
    for i in range(count // 2):
        here, beside = (pl.ds(((pair ^ i) + side) * slots, slots) for side in (0, count // 2))
        piece = slice(i * slots, (i + 1) * slots)
        rows_ref[here, near_at] = near_ref[piece]
        rows_ref[beside, near_at] = near_next[piece]
        rows_ref[here, far_at] = far_here[piece]
        rows_ref[beside, far_at] = far_next[piece]
    right = rows_ref[:, width:]
    gram_ref[:width, :] = prior_ref[:width, :] + dot(rows_ref[:, :width], rows_ref[...], 0, 0)
    gram_ref[width:, width:] = prior_ref[width:, width:] + dot(right, right, 0, 0)
    gram_ref[width:, :width] = jnp.zeros((width, width), jnp.float32)


def panel_gram(count, spot, parts, prior_gram):
    slots, total = parts[0].shape[0] * 2 // count, prior_gram.shape[0]
    return pl.pallas_call(
        functools.partial(panel_kernel, count),
        out_shape=(shape_of(count * slots, total), shape_of(total, total)),
        in_specs=[pl.BlockSpec(memory_space=pltpu.SMEM)] + [vmem_spec()] * 5,
        out_specs=(vmem_spec(),) * 2,
        compiler_params=params(),
        name="panel_gram",
    )(spot, *parts, prior_gram)


def gather_blocks(ref, first, rows, stride, blocks, work, at):
    for b in range(blocks):
        work[pl.ds(at, rows), b * LANES : (b + 1) * LANES] = ref[
            pl.ds(first + b, rows, stride=stride), :
        ]


def pack_kernel(first, each, joined, spot_ref, *refs):
    *sources, out_ref = refs
    outs = [out_ref] if len(out_ref.shape) == 2 else [out_ref.at[i] for i in range(2)]
    if joined:
        outs.pop(0)[...] = sources.pop(0)[...]
    for source, out in zip(sources, outs):
        slots, chunk, _ = source.shape
        flat = source.reshape(slots * chunk, LANES)
        for b in range(each):
            out[pl.ds(b, slots, stride=each), :] = flat[pl.ds(first + b, slots, stride=chunk), :]


def pack(spot, observed, part, each, sides, swapped_blocks=None):
    slots, rows, chunk, _ = observed.shape
    size = slots * each

    def source(side):
        at = lambda i, spot: (0, 2 * i + (spot[2] + side) % 2, 0, 0)
        return pl.BlockSpec((slots, None, chunk, LANES), at)

    specs, arrays = [source(side) for side in sides], [observed] * len(sides)
    if swapped_blocks is not None:
        specs = [pl.BlockSpec((None, size, LANES), lambda i, spot: (i, 0, 0))] + specs
        arrays = [swapped_blocks] + arrays
    if len(specs) == 1:
        out, out_spec = (rows // 2, size), pl.BlockSpec((None, size, LANES), lambda i, spot: (i, 0, 0))
    else:
        out = (rows // 2, 2, size)
        out_spec = pl.BlockSpec((None, 2, size, LANES), lambda i, spot: (i, 0, 0, 0))
    return pl.pallas_call(
        functools.partial(pack_kernel, part * each, each, swapped_blocks is not None),
        out_shape=shape_of(*out, LANES),
        grid_spec=pltpu.PrefetchScalarGridSpec(
            num_scalar_prefetch=1, grid=(rows // 2,), in_specs=specs, out_specs=out_spec
        ),
        compiler_params=params(),
        name="pack",
    )(spot, *arrays)


def plain_pack(spot, observed):
    slots, rows, chunk, _ = observed.shape
    pairs = observed.reshape(slots, rows // 2, 2, chunk, LANES).transpose(1, 2, 0, 3, 4)
    sides = [lax.dynamic_index_in_dim(pairs, (spot[2] + side) % 2, 1, keepdims=False) for side in (1, 0)]
    return jnp.stack(sides, axis=1).reshape(rows // 2, 2, slots * chunk, LANES)


def info_kernel(each, spot_ref, rows_ref, prior_ref, far_ref, near_ref, out_ref, work):
    count, pairs = rows_ref.shape[0], far_ref.shape[0]
    slots = count // 2 // pairs
    for i in range(pairs):
        gather_blocks(near_ref.at[i], 0, slots, each, each, work, i * slots)
        gather_blocks(far_ref.at[i], 0, slots, each, each, work, count // 2 + i * slots)
    out_ref[...] = prior_ref[...] + dot(rows_ref[...], work[...], 0, 0)


def info_part(part, each, spot, rows, prior_info, far, near):
    total = prior_info.shape[0]
    half = lambda array, at: pl.BlockSpec(
        (array.shape[0], None) + array.shape[2:], lambda i, spot: (0, at, 0, 0)
    )
    full = lambda array: pl.BlockSpec(array.shape, lambda i, spot: (0,) * array.ndim)
    return pl.pallas_call(
        functools.partial(info_kernel, each),
        out_shape=shape_of(total, each * LANES),
        grid_spec=pltpu.PrefetchScalarGridSpec(
            num_scalar_prefetch=1,
            grid=(1,),
            in_specs=[
                full(rows),
                pl.BlockSpec((total, each * LANES), lambda i, spot: (0, part)),
                full(far) if far.ndim == 3 else half(far, 0),
                half(near, 1),
            ],
            out_specs=pl.BlockSpec((total, each * LANES), lambda i, spot: (0, 0)),
            scratch_shapes=[pltpu.VMEM((rows.shape[0], each * LANES), jnp.float32)],
        ),
        compiler_params=params(),
        name="info_part",
    )(spot, rows, prior_info, far, near)


def slab_kernel(count, spot_ref, inverse_ref, own_ref, other_ref, out_ref):
    total, width = own_ref.shape
    own_rows, chunk = total // count, width // LANES
    half = total // 2
    tile = (own_rows, LANES)
    row_ids = lax.broadcasted_iota(jnp.int32, tile, 0)
    lane_ids = lax.broadcasted_iota(jnp.int32, tile, 1)
    info = own_ref[...] + other_ref[...]
    for side in range(2):
        depth = (side + 1) * half
        slab = dot(inverse_ref[side * half : depth, :depth], info[:depth, :], 1, 0)
        for b in range(chunk):
            for e in range(count // 2):
                d = side * (count // 2) + e
                part = slab[e * own_rows : (e + 1) * own_rows, b * LANES : (b + 1) * LANES]
                kept = jnp.where(spot_ref[SPOTS + b] + lane_ids >= row_ids + d * own_rows, part, 0.0)
                out_ref[d, pl.ds(b, own_rows, stride=chunk), :] = kept


def slab_part(count, spot, inverse, own, other):
    total, width = own.shape
    return pl.pallas_call(
        functools.partial(slab_kernel, count),
        out_shape=shape_of(count, total // count * width // LANES, LANES),
        in_specs=[pl.BlockSpec(memory_space=pltpu.SMEM)] + [vmem_spec()] * 3,
        out_specs=vmem_spec(),
        compiler_params=params(),
        name="slab_part",
    )(spot, inverse, own, other)


def sides_kernel(count, spot_ref, inverse_ref, own_ref, other_ref, near_ref, far_ref, work):
    total, width = own_ref.shape
    own_rows, chunk = total // count, width // LANES
    half = total // 2
    tile = (own_rows, LANES)
    row_ids = lax.broadcasted_iota(jnp.int32, tile, 0)
    lane_ids = lax.broadcasted_iota(jnp.int32, tile, 1)
    info = own_ref[...] + other_ref[...]
    for lower in range(2):
        depth = (lower + 1) * half
        work[lower * half : depth, :] = dot(inverse_ref[lower * half : depth, :depth], info[:depth, :], 1, 0)
    for change, out_ref in enumerate((near_ref, far_ref)):
        for pair in range(count // 2):
            first = pl.multiple_of((2 * pair + (spot_ref[2] + change) % 2) * own_rows, own_rows)
            for b in range(chunk):
                part = work[pl.ds(first, own_rows), b * LANES : (b + 1) * LANES]
                kept = jnp.where(spot_ref[SPOTS + b] + lane_ids >= row_ids + first, part, 0.0)
                out_ref[pair, pl.ds(b, own_rows, stride=chunk), :] = kept


def slab_sides(count, spot, inverse, own, other):
    total, width = own.shape
    out = shape_of(count // 2, total // count * width // LANES, LANES)
    return pl.pallas_call(
        functools.partial(sides_kernel, count),
        out_shape=(out, out),
        in_specs=[pl.BlockSpec(memory_space=pltpu.SMEM)] + [vmem_spec()] * 3,
        out_specs=(vmem_spec(),) * 2,
        scratch_shapes=[pltpu.VMEM((total, width), jnp.float32)],
        compiler_params=params(),
        name="slab_sides",
    )(spot, inverse, own, other)


def swapped(value, axis, bits):
    count = lax.axis_size(axis)
    return lax.ppermute(value, axis, [(i, i ^ bits) for i in range(count)])


def handed_on(value):
    return lax.ppermute(value, "section", [(0, 1)])


def z_panels(near):
    rows = lax.axis_size("row")
    return jnp.concatenate([near] + [swapped(near, "row", k) for k in range(2, rows, 2)], axis=0)


def prior_panels(near_prior):
    if lax.axis_size("col") == 2:
        return near_prior, swapped(near_prior, "col", 1)
    priors = lax.all_gather(near_prior, "col")
    return priors[0], priors[1]


def all_panels(near):
    rows, cols = lax.axis_size("row"), lax.axis_size("col")
    if cols == 2:
        order = [(i, i ^ 3) for i in range(rows * cols)]
        far = [swapped(near, "col", 1), lax.ppermute(near, ("row", "col"), order)]
        return [near, swapped(near, "row", 1)] + far
    both = lax.all_gather(near, "col")
    both = [both[0], both[1]]
    beside = [swapped(panel, "row", 1) for panel in both]
    return [both[0], beside[0], both[1], beside[1]]


def on_device(prior_root, observations, live_rows):
    total, cycles, _, width = prior_root.shape
    slots = observations.shape[1]
    rows, cols = lax.axis_size("row"), lax.axis_size("col")
    per = width // LANES
    blocks = cycles * per
    chunk = -(-blocks // rows)
    parts = 2 if chunk % GROUP == 0 else 1
    each = chunk // parts
    col, row, section = (lax.axis_index(axis) for axis in ("col", "row", "section"))
    group = min(GROUP, chunk * rows)

    def spot_of(part):
        first = row * chunk + part * each
        spot = [col if cols == 2 else 0, section, row, 0, first // group, first % group]
        spot += [((first + b) // per * cols + col) * width + (first + b) % per * LANES for b in range(each)]
        return jnp.stack([jnp.asarray(value, jnp.int32) for value in spot])

    def in_blocks(array):
        array = array.reshape(array.shape[0], blocks, LANES)
        return jnp.pad(array, ((0, 0), (0, chunk * rows - blocks), (0, 0)))

    spots = [spot_of(part) for part in range(parts)]
    prior = in_blocks(prior_root.reshape(total, -1)).reshape(total, -1, group, LANES)
    observed = in_blocks(observations.reshape(slots, -1)).reshape(slots, rows, chunk, LANES)
    live = lax.broadcasted_iota(jnp.int32, (slots, 1), 0) < live_rows[0, 0]
    near = jnp.where(live, observations[0, :, 0, 0, :], 0.0)
    same_side = [[2 * i + side for i in range(rows // 2)] for side in range(2)]

    def over(piece):
        return lax.all_to_all(piece, "row", 0, 0, axis_index_groups=same_side, tiled=True)

    near = z_panels(near)
    priors = prior_panels(prior_root[:, 0, 0, :])
    if parts > 1:
        crossing = pack(spots[0], observed, 1, each, [1])
        packed = pack(spots[0], observed, 0, each, [1, 0])
        packed, crossing, near = lax.optimization_barrier((packed, crossing, near))
        crossed = swapped(crossing, "row", 1)
        near, priors = lax.optimization_barrier((near, priors))
    else:
        packed, near = lax.optimization_barrier((plain_pack(spots[0], observed), near))
    panels = all_panels(near)
    first = over(packed)
    far = first[:, 0]
    far, _ = lax.optimization_barrier((far, panels))
    arrived = [(swapped(far, "row", 1), first)]
    prior_info, prior_gram = prior_part(chunk, spots[0], *priors, prior)
    if parts > 1:
        observed, prior_gram = lax.optimization_barrier((observed, prior_gram))
        packed = pack(spots[0], observed, 1, each, [0], crossed)
        packed, panels = lax.optimization_barrier((packed, panels))
    rows_panel, gram = panel_gram(rows, spots[0], panels, prior_gram)
    other_gram = handed_on(gram)
    if parts > 1:
        packed, first = lax.optimization_barrier((packed, first))
        second = over(packed)
        arrived.append((second, second))
    inverse = factor(gram, other_gram)
    rows_panel, inverse = lax.optimization_barrier((rows_panel, inverse))
    out = jnp.zeros((total // rows, rows, parts, each, LANES), jnp.float32)
    for part, (far, near) in enumerate(arrived):
        if part:
            rows_panel, other = lax.optimization_barrier((rows_panel, other))
        info = info_part(part, each, spots[part], rows_panel, prior_info, far, near)
        other = handed_on(info)
        if part == 0:
            slab = slab_part(rows, spots[part], inverse, info, other)
            slab = lax.all_to_all(slab, "row", 0, 0, tiled=True)
            continue
        sides = slab_sides(rows, spots[part], inverse, info, other)
        placed = []
        for change, side in enumerate(sides):
            for k in range(rows // 2):
                piece = lax.dynamic_index_in_dim(side, (row // 2) ^ k, 0, keepdims=False)
                piece = swapped(piece, "row", 2 * k + change) if 2 * k + change else piece
                placed.append((row ^ (2 * k + change), piece.reshape(total // rows, each, LANES)))
        slab, received = lax.optimization_barrier((slab, [piece for _, piece in placed]))
        placed = [(source, piece) for (source, _), piece in zip(placed, received)]
    slab = slab.reshape(rows, total // rows, each, LANES).transpose(1, 0, 2, 3)
    out = out.at[:, :, 0].set(slab)
    if parts > 1:
        out = out.reshape(total // rows, rows * parts, each, LANES)
        for source, piece in placed:
            out = lax.dynamic_update_index_in_dim(out, piece, source * parts + 1, 1)
    out = out.reshape(total // rows, rows * chunk, LANES)[:, :blocks]
    return out.reshape(1, total // rows, cycles, 1, width)


def solution(mesh):
    placed = (
        P(None, None, "col", None),
        P("section", "row", None, "col", None),
        P("section", "row"),
    )
    return jax.shard_map(
        on_device,
        mesh=mesh,
        in_specs=placed,
        out_specs=P("section", "row", None, "col", None),
        check_vma=False,
    )
```
